256 devices in a mesh: dp: 8 (over z), fsdp: 32 (over x, y, core).
Axes of the slice: x: 4, y: 4, z: 8, core: 2. Of those that a mesh axis runs over, the one named last changes fastest.
Arguments:
- query_key_value: bfloat16 [131584, 4992], P(('dp', 'fsdp')), may hold values from -6 to 6
- cotangent: bfloat16 [131584, 3200], P(('dp', 'fsdp')), may hold values from -24 to 24
- output_weight: bfloat16 [1664, 3200], P(None, 'fsdp'), may hold values from -0.15625 to 0.15625
- layer_scale: bfloat16 [3200], P('fsdp'), may hold values from 0.25 to 4
- tile_counts: int32 [256], replicated, may hold values from 1 to 2, as said below
Outputs:
- grad_inputs: bfloat16 [131584, 3328], P(('dp', 'fsdp'))
- grad_weight: float32 [1664, 3200], P(None, 'fsdp')
- grad_scale: float32 [3200], P('fsdp')
The draws below stay inside these ranges and needn't reach their ends.
Inputs may be any that keep to these rules, and one draw needn't show every extreme that they name: `tile_counts`: A device and the device 32 // 2 fsdp places away in the same data group hold at most 3 live tiles together; the live tiles of a device are its first slots.
All inputs are finite; a program needn't handle non-finite values.
Results may differ from the reference program's by a relative error of at most 0.029.
Values may be sent and summed in bfloat16 or wider, within the bound.
A program may use at most 192 MiB of HBM per device.

```python
import math
import jax
import jax.numpy as jnp
from jax import lax

D = 3200
HEADS = 13
HEAD_DIM = 128
TILE = 257
SLOTS = 2
ROWS = 131584
N_DP = 8
N_FSDP = 32


def draw_query_key_value(key, part):
    key = jax.random.fold_in(key, 7)
    head_width = HEADS * HEAD_DIM
    sample_rows = jax.random.truncated_normal(key, -6.0, 6.0, (ROWS, 3 * head_width), jnp.float32)
    return sample_rows.astype(jnp.bfloat16)


def draw_tile_counts(key, part):
    key = jax.random.fold_in(key, 13)
    half_axis = N_FSDP // 2
    first_key, second_key, flip_key = jax.random.split(key, 3)
    leading = jax.random.randint(first_key, (N_DP, half_axis), 1, SLOTS + 1)
    leading = leading.at[:, 0].set(SLOTS)
    room = SLOTS + 1 - leading
    trailing = jax.random.randint(second_key, (N_DP, half_axis), 0, 1 << 20) % room + 1
    flipped = jax.random.randint(flip_key, (N_DP, half_axis), 0, 2) == 1
    lower = jnp.where(flipped, trailing, leading)
    upper = jnp.where(flipped, leading, trailing)
    return jnp.concatenate([lower, upper], axis=1).reshape(N_DP * N_FSDP).astype(jnp.int32)


def with_spikes(values, key, source, target, blocks, factor):
    owner, partner = [(jnp.arange(values.shape[dim]) // (values.shape[dim] // blocks)).reshape([-1 if axis == dim else 1 for axis in range(values.ndim)]) for dim in (source, target)]
    chosen = jax.random.permutation(key, blocks)[partner]
    strong = (owner == chosen) | (owner == (partner + blocks // 2) % blocks)
    return jnp.where(strong, factor * values, values)


def steps_of(rng, dims, shards, low, largest):
    level = 1.0
    for dim, shards_of in shards:
        draws = jax.random.uniform(jax.random.fold_in(jax.random.fold_in(rng, 6), dim), (shards_of,), jnp.float32, low / len(shards), largest / len(shards))
        level = level * jnp.repeat(jnp.exp(draws), dims[dim] // shards_of).reshape((-1,) + (1,) * (len(dims) - 1 - dim))
    return level


def scatter_about(key, shape, deviation, reach, shards=(), held_as=jnp.bfloat16):
    loudness = steps_of(key, shape, shards, -0.22, 0.18) if shards else 1.0
    values = jax.random.normal(key, shape, jnp.float32) * deviation * loudness
    return jnp.minimum(jnp.maximum(values, -reach), reach).astype(held_as)


def gaussian_with(stream_key, extent, scale, reach, shards, heavy, kind=jnp.bfloat16):
    values = scale * jax.random.normal(stream_key, extent, jnp.float32)
    if shards:
        values = values * steps_of(stream_key, extent, shards, -0.22, 0.18)
    return jnp.clip(with_spikes(values, jax.random.fold_in(stream_key, 3), *heavy), -reach, reach).astype(kind)


def setup_inputs(seed: int = 0) -> dict:
    arg_keys = jax.random.split(jax.random.key(seed), 6)
    return {
        "query_key_value": draw_query_key_value(jax.random.fold_in(arg_keys[5], 71), 0),
        "cotangent": gaussian_with(arg_keys[1], (ROWS, D), 1.0, 24.0, ((0, 256),), (0, 1, 128, 5.5)),
        "output_weight": scatter_about(arg_keys[2], (HEADS * HEAD_DIM, D), (HEADS * HEAD_DIM) ** -0.5, 0.15625, ((1, 32),)),
        "layer_scale": jnp.clip(jnp.exp(math.log(4.0) - 2.7725887 * jax.random.uniform(arg_keys[3], (D,), jnp.float32) ** steps_of(arg_keys[3], (D,), ((0, 32),), -0.2, 0.2)), 0.25, 4.0).astype(jnp.bfloat16),
        "tile_counts": draw_tile_counts(jax.random.fold_in(arg_keys[5], 71), 0),
    }


def tile_grads(inputs_tile, scaled_tile, weight):
    length = inputs_tile.shape[0]
    head_width = weight.shape[0]
    head_count = head_width // HEAD_DIM
    inverse = 1.0 / math.sqrt(HEAD_DIM)
    queries = inputs_tile[:, :head_width].reshape(length, head_count, HEAD_DIM).astype(jnp.float32)
    key_rows = inputs_tile[:, head_width:2 * head_width].reshape(length, head_count, HEAD_DIM).astype(jnp.float32)
    value_rows = inputs_tile[:, 2 * head_width:].reshape(length, head_count, HEAD_DIM).astype(jnp.float32)
    scores = jnp.einsum('qhd,khd->hqk', queries, key_rows) * inverse
    probs = jax.nn.softmax(scores, axis=-1).astype(jnp.bfloat16)
    prob_float = probs.astype(jnp.float32)
    attended = jnp.einsum('hqk,khd->qhd', prob_float, value_rows).reshape(length, head_width).astype(jnp.bfloat16)
    d_attended = lax.dot_general(scaled_tile, weight, (((1,), (1,)), ((), ())), preferred_element_type=jnp.float32).astype(jnp.bfloat16)
    d_heads = d_attended.reshape(length, head_count, HEAD_DIM).astype(jnp.float32)
    d_probs = jnp.einsum('qhd,khd->hqk', d_heads, value_rows)
    d_scores = (prob_float * (d_probs - lax.optimization_barrier(jnp.sum(d_probs * prob_float, axis=-1, keepdims=True))) * inverse).astype(jnp.bfloat16)
    score_float = d_scores.astype(jnp.float32)
    grad_query = jnp.einsum('hqk,khd->qhd', score_float, key_rows).reshape(length, head_width)
    grad_key = jnp.einsum('hqk,qhd->khd', score_float, queries).reshape(length, head_width)
    result = jnp.concatenate([grad_query, grad_key], axis=1).astype(jnp.bfloat16)
    return (result, attended)

def reference(query_key_value, cotangent, output_weight, layer_scale, tile_counts):
    head_width = HEADS * HEAD_DIM
    devices_all = N_DP * N_FSDP
    inputs_all = query_key_value.reshape(devices_all, SLOTS, TILE, 3 * head_width)
    grads_all = cotangent.reshape(devices_all, SLOTS, TILE, D)
    gain_full = layer_scale.astype(jnp.float32)

    def device_step(carried, packed):
        inputs_dev, grads_dev, live_count = packed
        scaled_grad = (gain_full * grads_dev.astype(jnp.float32)).astype(jnp.bfloat16)
        grad_inputs, attended = jax.vmap(lambda first, third: tile_grads(first, third, output_weight))(inputs_dev, scaled_grad)
        live_mask = jnp.arange(SLOTS, dtype=jnp.int32) < live_count
        grad_inputs = jnp.where(live_mask[:, None, None], grad_inputs, jnp.zeros_like(grad_inputs))
        attended = jnp.where(live_mask[:, None, None], attended, jnp.zeros_like(attended))
        partial_weight = jnp.dot(attended.reshape(-1, head_width).T, grads_dev.reshape(-1, D), preferred_element_type=jnp.float32)
        partial_weight = lax.optimization_barrier(partial_weight.astype(jnp.bfloat16)).astype(jnp.float32)
        return (carried + partial_weight, grad_inputs)
    start = jnp.zeros((head_width, D), jnp.float32)
    summed, grad_inputs = lax.scan(device_step, start, (inputs_all, grads_all, tile_counts))
    factor = 8.0 / math.sqrt(ROWS)
    grad_weight = factor * gain_full[None, :] * summed
    grad_scale = factor * lax.optimization_barrier(jnp.sum(output_weight.astype(jnp.float32) * summed, axis=0))
    return (grad_inputs.reshape(ROWS, 2 * head_width), grad_weight, grad_scale)
```

```python
import functools
import math

import jax
import jax.numpy as jnp
from jax import lax
from jax.experimental import pallas as pl
from jax.experimental.pallas import tpu as pltpu
from jax.sharding import PartitionSpec as P

HEAD_DIM = 128
TILE = 257
SLOTS = 2
HEADS = 13
WIDTH = HEADS * HEAD_DIM
MODEL = 3200
SHARD = 100
PADDED = 112
N_FSDP = 32
N_DP = 8
ROWS_DEV = SLOTS * TILE
WINDOW = 258
STARTS = (0, 256)
LANES = ((0, 896), (896, 768))
TOP = 64
BOTTOM = PADDED - TOP
PIECE = 16
MIB = 1024 * 1024
F32 = jnp.float32
BF16 = jnp.bfloat16
MESH = pl.DeviceIdType.MESH


def dot(a, b, dims):
    return lax.dot_general(a, b, (dims, ((), ())), preferred_element_type=F32)


def selection(tile, transposed):
    first = 128 * tile
    owner = first // PADDED
    base = owner * SHARD + jnp.minimum(first - owner * PADDED, SHARD - 1)
    source_tile = jnp.minimum(base // 128, MODEL // 128 - 2)
    shape = (128, 256) if transposed else (256, 128)
    target = lax.broadcasted_iota(jnp.int32, shape, 0 if transposed else 1) + first
    source = lax.broadcasted_iota(jnp.int32, shape, 1 if transposed else 0) + source_tile * 128
    chosen = jnp.zeros(shape, F32)
    for step in range(3):
        index = owner + step
        inside = (target >= index * PADDED) & (target < index * PADDED + SHARD)
        chosen = jnp.where(inside & (source == target - index * (PADDED - SHARD)), 1.0, chosen)
    columns = pl.ds(pl.multiple_of(source_tile * 128, 128), 256)
    return chosen.astype(BF16), columns


def spread_cotangent(cot_ref, padded_ref):
    def one_tile(tile, carry):
        chooser, source = selection(tile, False)
        columns = pl.ds(pl.multiple_of(tile * 128, 128), 128)
        padded_ref[:, columns] = dot(cot_ref[:, source], chooser, ((1,), (0,))).astype(BF16)
        return carry

    lax.fori_loop(0, N_FSDP * PADDED // 128, one_tile, 0)


def head_probs(queries, keys, slot):
    scores = dot(queries, keys, ((1,), (1,)))
    column = lax.broadcasted_iota(jnp.int32, scores.shape, 1)
    row = lax.broadcasted_iota(jnp.int32, scores.shape, 0)
    out_of_tile = WINDOW - 1 if slot == 0 else 0
    scores = jnp.where(column == out_of_tile, -1e30, scores)
    top = jnp.max(scores, axis=1, keepdims=True)
    powers = jnp.exp((scores - top) * (1.0 / math.sqrt(HEAD_DIM)))
    total = jnp.sum(powers, axis=1, keepdims=True)
    probs = powers * (1.0 / total)
    return jnp.where(row == out_of_tile, 0.0, probs).astype(BF16)


def store_window(ref, slot, columns, values):
    if slot == 0:
        ref[0:WINDOW, columns] = values
    else:
        kept = ref[256:272, columns]
        row = lax.broadcasted_iota(jnp.int32, kept.shape, 0)
        ref[256 : 256 + WINDOW, columns] = values
        ref[256:272, columns] = jnp.where(row == 0, kept, values[0:16])


def head_columns(third, head):
    return pl.ds(pl.multiple_of(third * WIDTH + head * HEAD_DIM, 128), HEAD_DIM)


def forward_heads(qkv_ref, live_ref, attended_ref, probs_ref, slots):
    for slot in slots:
        rows = slice(STARTS[slot], STARTS[slot] + WINDOW)

        def one_head(head, carry, slot=slot, rows=rows):
            queries = qkv_ref[rows, head_columns(0, head)]
            keys = qkv_ref[rows, head_columns(1, head)]
            values = qkv_ref[rows, head_columns(2, head)]
            probs = head_probs(queries, keys, slot)
            if probs_ref is not None:
                probs_ref[slot * HEADS + head] = probs
            attended = dot(probs, values, ((1,), (0,)))
            attended = jnp.where(live_ref[slot : slot + 1, :] > 0.5, attended, 0.0).astype(BF16)
            store_window(attended_ref, slot, head_columns(0, head), attended)
            return carry

        lax.fori_loop(0, HEADS, one_head, 0)


def weight_partials(cot_ref, attended_ref, turned_ref, partial_ref):
    tiles = N_FSDP * PADDED // 4 // 128

    def one_line(line, carry):
        def one_tile(tile, inner):
            chooser, source = selection(line * tiles + tile, True)
            rows = pl.ds(pl.multiple_of(tile * 128, 128), 128)
            turned_ref[rows, :] = dot(chooser, cot_ref[:, source], ((1,), (1,))).astype(BF16)
            return inner

        lax.fori_loop(0, tiles, one_tile, 0)
        for start in range(0, WIDTH, 256):
            size = min(256, WIDTH - start)
            columns = slice(start, start + size)
            sums = dot(turned_ref[...], attended_ref[:, columns], ((1,), (0,)))
            partial_ref[line, :, :, :, columns] = sums.astype(BF16).reshape(4, 2, PADDED, size)
        return carry

    lax.fori_loop(0, 4, one_line, 0)


def attended_grads(padded_ref, weight_ref, d_attended_ref, first, last):
    def one_block(columns, size):
        right = weight_ref[:, :, :, :, columns].reshape(N_FSDP * PADDED, size)
        d_attended_ref[:, columns] = dot(padded_ref[...], right, ((1,), (0,))).astype(BF16)

    def one_full(index, carry):
        one_block(pl.ds(pl.multiple_of(index * 256, 256), 256), 256)
        return carry

    lax.fori_loop(first, min(last, WIDTH // 256), one_full, 0)
    if last > WIDTH // 256 and WIDTH % 256:
        one_block(slice(WIDTH // 256 * 256, WIDTH), WIDTH % 256)


def backward_heads(qkv_ref, live_ref, probs_ref, d_attended_ref, grad_ref, slot, first, last):
    inverse = 1.0 / math.sqrt(HEAD_DIM)
    if True:
        rows = slice(STARTS[slot], STARTS[slot] + WINDOW)

        def one_head(head, carry, slot=slot, rows=rows):
            queries = qkv_ref[rows, head_columns(0, head)]
            keys = qkv_ref[rows, head_columns(1, head)]
            values = qkv_ref[rows, head_columns(2, head)]
            if probs_ref is None:
                probs = head_probs(queries, keys, slot).astype(F32)
            else:
                probs = probs_ref[slot * HEADS + head].astype(F32)
            live = live_ref[slot : slot + 1, :] > 0.5
            d_probs = dot(d_attended_ref[rows, head_columns(0, head)], values, ((1,), (1,)))
            weighted = jnp.sum(d_probs * probs, axis=1, keepdims=True)
            d_scores = (probs * ((d_probs - weighted) * inverse)).astype(BF16)
            grad_query = jnp.where(live, dot(d_scores, keys, ((1,), (0,))), 0.0).astype(BF16)
            grad_key = jnp.where(live, dot(d_scores, queries, ((0,), (0,))), 0.0).astype(BF16)
            store_window(grad_ref, slot, head_columns(0, head), grad_query)
            store_window(grad_ref, slot, head_columns(1, head), grad_key)
            return carry

        lax.fori_loop(min(first, HEADS), min(last, HEADS), one_head, 0)


class Copies:
    def __init__(self, send_sems, recv_sems):
        self.send_sems, self.recv_sems, self.count, self.made = send_sems, recv_sems, 0, []

    def start(self, source, target, device):
        copy = pltpu.make_async_remote_copy(
            src_ref=source,
            dst_ref=target,
            send_sem=self.send_sems.at[self.count],
            recv_sem=self.recv_sems.at[self.count],
            device_id=device,
            device_id_type=MESH,
        )
        copy.start()
        self.count += 1
        self.made.append(copy)
        return copy

    def finish(self):
        for copy in self.made:
            copy.wait_send()


class Place:
    def __init__(self):
        self.f = lax.axis_index("fsdp")
        self.z = lax.axis_index("dp")
        self.c = lax.rem(self.f, 2)
        chip = self.f // 2
        self.y = lax.rem(chip, 4)
        self.x = chip // 4

    def device(self, x, y, c):
        return (self.z, ((x * 4) + y) * 2 + c)

    def around(self, axis, steps):
        u = lax.rem((self.x if axis == 0 else self.y) + 4 + steps, 4)
        return u

    def neighbour(self, axis, steps):
        u = self.around(axis, steps)
        return self.device(u, self.y, self.c) if axis == 0 else self.device(self.x, u, self.c)

    def sibling(self):
        return self.device(self.x, self.y, 1 - self.c)

    def layer(self, steps):
        return lax.rem(self.z + steps, N_DP)

    def greet(self):
        barrier = pltpu.get_barrier_semaphore()
        others = [self.sibling()]
        for axis in (0, 1):
            for step in (1, -1):
                others.append(self.neighbour(axis, step))
        for step in range(1, N_DP):
            others.append((self.layer(step), self.f))
        for other in others:
            pl.semaphore_signal(barrier, inc=1, device_id=other, device_id_type=MESH)
        pl.semaphore_wait(barrier, len(others))


def pick(first, u, v):
    return (u, v) if first == 0 else (v, u)


class WeightGather:
    def __init__(self, place, copies, weight_ref):
        self.place, self.copies, self.weight = place, copies, weight_ref
        self.own = (place.x, place.y)

    def block(self, half, x, y, rows=slice(0, PADDED)):
        start, size = LANES[half]
        return self.weight.at[x, y, self.place.c, rows, slice(start, start + size)]

    def send(self, half, axis, step, x, y, rows=slice(0, PADDED)):
        ref = self.block(half, x, y, rows)
        return self.copies.start(ref, ref, self.place.neighbour(axis, step))

    def begin(self):
        self.first = {}
        self.second = {}
        for half in (0, 1):
            for step in (1, -1):
                self.first[half, step] = self.send(half, half, step, *self.own)
        for half in (0, 1):
            self.send_second(half, 0)

    def send_second(self, half, away):
        u, v = self.place.around(half, away), self.place.around(1 - half, 0)
        for step in (1, -1):
            self.second[half, away, step] = self.send(half, 1 - half, step, *pick(half, u, v))

    def middle(self):
        self.far = {}
        place = self.place
        for step in (1, -1):
            for half in (0, 1):
                self.first[half, step].wait_recv()
                u, v = place.around(half, -step), place.around(1 - half, 0)
                part = slice(0, TOP) if step == 1 else slice(TOP, PADDED)
                self.far[half, step] = self.send(half, half, step, *pick(half, u, v), part)
                self.send_second(half, -step)
        for half in (0, 1):
            for step in (1, -1):
                self.far[half, step].wait_recv()
            self.send_second(half, 2)

    def spread(self):
        place = self.place
        self.last = {}
        for away in (0, -1, 1, 2):
            for half in (0, 1):
                for step in (1, -1):
                    self.second[half, away, step].wait_recv()
                    u, v = place.around(half, away), place.around(1 - half, -step)
                    part = slice(0, TOP) if step == 1 else slice(TOP, PADDED)
                    self.last[half, away, step] = self.send(
                        half, 1 - half, step, *pick(half, u, v), part
                    )

    def share(self):
        place = self.place
        self.shared = []
        for away in (0, -1, 1, 2):
            for half in (0, 1):
                for step in (1, -1):
                    self.last[half, away, step].wait_recv()
                u = place.around(half, away)
                start, size = LANES[half]
                line = (u, slice(None)) if half == 0 else (slice(None), u)
                ref = self.weight.at[*line, place.c, :, slice(start, start + size)]
                self.shared.append(self.copies.start(ref, ref, place.sibling()))

    def end(self):
        for copy in self.shared:
            copy.wait_recv()


class GradReduce:
    def __init__(self, place, copies, partial_ref, sums_ref, buffers, layers_ref, result_ref):
        self.place, self.copies = place, copies
        self.partial, self.sums, self.buffers = partial_ref, sums_ref, buffers
        self.layers, self.result = layers_ref, result_ref

    def line(self, half, away):
        u = self.place.around(half, away)
        return (u, slice(None)) if half == 0 else (slice(None), u)

    def lanes(self, half):
        return slice(LANES[half][0], LANES[half][0] + LANES[half][1])

    def begin(self):
        self.crossed = {}
        for away in (2, 1, -1, 0):
            for half in (0, 1):
                line, lanes = self.line(half, away), self.lanes(half)
                self.crossed[half, away] = self.copies.start(
                    self.partial.at[*line, 1 - self.place.c, :, lanes],
                    self.sums.at[*line, :, lanes],
                    self.place.sibling(),
                )

    def chunk(self, half, away, v):
        u = self.place.around(half, away)
        return pick(half, u, v)

    def add_own(self, half, away):
        self.crossed[half, away].wait_recv()
        lanes = self.lanes(half)

        def one(v, carry):
            x, y = self.chunk(half, away, v)
            total = self.sums[x, y, :, lanes].astype(F32)
            total += self.partial[x, y, self.place.c, :, lanes].astype(F32)
            self.sums[x, y, :, lanes] = total.astype(BF16)
            return carry

        lax.fori_loop(0, 4, one, 0)

    def group(self, half, away, first):
        u = self.place.around(half, away)
        part = slice(first, first + 2)
        return self.sums.at[*pick(half, u, part), :, self.lanes(half)]

    def first_sends(self):
        self.near, self.far = {}, {}
        place = self.place
        for half in (0, 1):
            self.add_own(half, 2)
            for step in (1, -1):
                self.far[half, step] = self.copies.start(
                    self.group(half, 2, 0 if step == 1 else 2),
                    self.buffers[half][0].at[0 if step == 1 else 1],
                    place.neighbour(half, step),
                )
        for step in (1, -1):
            for half in (0, 1):
                self.add_own(half, step)
                other = 2 if step == 1 else 0
                self.near[half, step, 0] = self.copies.start(
                    self.group(half, step, other),
                    self.buffers[half][1].at[0 if step == 1 else 1, slice(other, other + 2)],
                    place.neighbour(half, step),
                )
        for half in (0, 1):
            self.add_own(half, 0)

    def first_forward(self):
        place = self.place
        for step in (1, -1):
            for half in (0, 1):
                side, start = (0, 0) if step == 1 else (1, 2)
                self.far[half, step].wait_recv()
                lanes = self.lanes(half)
                arrived = self.buffers[half][0]

                def one(v, carry, half=half, side=side, start=start, lanes=lanes, arrived=arrived):
                    x, y = self.chunk(half, step, start + v)
                    total = self.sums[x, y, :, lanes].astype(F32)
                    total += arrived[side, v].astype(F32)
                    self.sums[x, y, :, lanes] = total.astype(BF16)
                    return carry

                lax.fori_loop(0, 2, one, 0)
                self.near[half, step, 1] = self.copies.start(
                    self.group(half, step, start),
                    self.buffers[half][1].at[side, slice(start, start + 2)],
                    place.neighbour(half, step),
                )

    def first_end(self):
        for half in (0, 1):
            for step in (1, -1):
                self.near[half, step, 0].wait_recv()
                self.near[half, step, 1].wait_recv()
            lanes = self.lanes(half)
            arrived = self.buffers[half][1]

            def one(v, carry, half=half, lanes=lanes, arrived=arrived):
                x, y = self.chunk(half, 0, v)
                total = self.sums[x, y, :, lanes].astype(F32)
                total += arrived[0, v].astype(F32) + arrived[1, v].astype(F32)
                self.sums[x, y, :, lanes] = total.astype(BF16)
                return carry

            lax.fori_loop(0, 4, one, 0)
            self.second_sends(half)

    def mine(self, half, away):
        place = self.place
        return pick(half, place.around(half, 0), place.around(1 - half, away))

    def second_sends(self, half):
        place, lanes = self.place, self.lanes(half)
        if half == 0:
            self.far2, self.near2 = {}, {}
        for step in (1, -1):
            side = 0 if step == 1 else 1
            rows = slice(0, TOP) if step == 1 else slice(TOP, PADDED)
            self.far2[half, step] = self.copies.start(
                self.sums.at[*self.mine(half, 2), rows, lanes],
                self.buffers[half][2].at[side, rows],
                place.neighbour(1 - half, step),
            )
        for step in (1, -1):
            side = 0 if step == 1 else 1
            rows = slice(TOP, PADDED) if step == 1 else slice(0, TOP)
            self.near2[half, step, 0] = self.copies.start(
                self.sums.at[*self.mine(half, step), rows, lanes],
                self.buffers[half][3].at[side, rows],
                place.neighbour(1 - half, step),
            )

    def second_forward(self):
        place = self.place
        for half in (0, 1):
            lanes = self.lanes(half)
            for step in (1, -1):
                side = 0 if step == 1 else 1
                rows = slice(0, TOP) if step == 1 else slice(TOP, PADDED)
                self.far2[half, step].wait_recv()
                x, y = self.mine(half, step)
                total = self.sums[x, y, rows, lanes].astype(F32)
                total += self.buffers[half][2][side, rows].astype(F32)
                self.sums[x, y, rows, lanes] = total.astype(BF16)
                self.near2[half, step, 1] = self.copies.start(
                    self.sums.at[x, y, rows, lanes],
                    self.buffers[half][3].at[side, rows],
                    place.neighbour(1 - half, step),
                )

    def second_end(self):
        layers = self.layers
        layers[0, PADDED:128, :] = jnp.zeros((128 - PADDED, WIDTH), BF16)
        for half in (0, 1):
            lanes = self.lanes(half)
            for step in (1, -1):
                self.near2[half, step, 0].wait_recv()
                self.near2[half, step, 1].wait_recv()
            x, y = self.mine(half, 0)
            arrived = self.buffers[half][3]
            total = self.sums[x, y, :, lanes].astype(F32)
            total += arrived[0].astype(F32) + arrived[1].astype(F32)
            layers[0, 0:PADDED, lanes] = total.astype(BF16)

    def piece(self, z):
        return pl.ds(pl.multiple_of(z * PIECE, PIECE), PIECE)

    def layer_sends(self):
        place = self.place
        self.up = [
            self.copies.start(
                self.layers.at[0, self.piece(place.layer(step))],
                self.layers.at[1, slice(step * PIECE, step * PIECE + PIECE)],
                (place.layer(step), place.f),
            )
            for step in range(1, N_DP)
        ]

    def layer_sums(self):
        place = self.place
        own = self.piece(place.z)
        total = self.layers[0, own, :].astype(F32)
        for step in range(1, N_DP):
            self.up[step - 1].wait_recv()
            total += self.layers[1, step * PIECE : step * PIECE + PIECE, :].astype(F32)
        self.result[own, :] = total.astype(BF16)
        self.down = [
            self.copies.start(
                self.result.at[own], self.result.at[own], (place.layer(step), place.f)
            )
            for step in range(1, N_DP)
        ]

    def end(self):
        for copy in self.down:
            copy.wait_recv()


N_COPIES = 48 + 8 + 12 + 12 + 14


def whole_kernel(
    shard_ref, qkv_ref, cot_ref, live_ref, grad_ref, result_ref, weight_ref, partial_ref, sums_ref,
    b00, b01, b02, b03, b10, b11, b12, b13, layers_ref, padded_ref, turned_ref, attended_ref,
    probs_ref, send_sems, recv_sems,
):
    place = Place()
    copies = Copies(send_sems, recv_sems)
    weight_ref[place.x, place.y, place.c] = shard_ref[...]
    place.greet()
    gather = WeightGather(place, copies, weight_ref)
    reduce = GradReduce(
        place, copies, partial_ref, sums_ref, ((b00, b01, b02, b03), (b10, b11, b12, b13)),
        layers_ref, result_ref,
    )

    def backward(slot, first, last):
        backward_heads(
            qkv_ref, live_ref, probs_ref, attended_ref, grad_ref, slot, first, last
        )

    gather.begin()
    forward_heads(qkv_ref, live_ref, attended_ref, probs_ref, (0,))
    gather.middle()
    forward_heads(qkv_ref, live_ref, attended_ref, probs_ref, (1,))
    gather.spread()
    weight_partials(cot_ref, attended_ref, turned_ref, partial_ref)
    reduce.begin()
    gather.share()
    spread_cotangent(cot_ref, padded_ref)
    gather.end()
    reduce.first_sends()
    attended_grads(padded_ref, weight_ref, attended_ref, 0, 7)
    reduce.first_forward()
    backward(0, 0, 7)
    reduce.first_end()
    backward(0, 7, 10)
    reduce.second_forward()
    backward(0, 10, HEADS)
    reduce.second_end()
    reduce.layer_sends()
    backward(1, 0, 6)
    reduce.layer_sums()
    backward(1, 6, HEADS)
    reduce.end()
    copies.finish()


def exchange_buffers():
    shapes = []
    for _, size in LANES:
        shapes += [
            pltpu.VMEM((2, 2, PADDED, size), BF16),
            pltpu.VMEM((2, 4, PADDED, size), BF16),
            pltpu.VMEM((2, PADDED, size), BF16),
            pltpu.VMEM((2, PADDED, size), BF16),
        ]
    return shapes


VMEM = pl.BlockSpec(memory_space=pltpu.VMEM)


def whole(shard, qkv, cot, live):
    return pl.pallas_call(
        whole_kernel,
        out_shape=(
            jax.ShapeDtypeStruct((ROWS_DEV, 2 * WIDTH), BF16),
            jax.ShapeDtypeStruct((128, WIDTH), BF16),
        ),
        in_specs=[VMEM] * 4,
        out_specs=[VMEM] * 2,
        scratch_shapes=[
            pltpu.VMEM((4, 4, 2, PADDED, WIDTH), BF16),
            pltpu.VMEM((4, 4, 2, PADDED, WIDTH), BF16),
            pltpu.VMEM((4, 4, PADDED, WIDTH), BF16),
        ]
        + exchange_buffers()
        + [
            pltpu.VMEM((2, 128, WIDTH), BF16),
            pltpu.VMEM((ROWS_DEV, N_FSDP * PADDED), BF16),
            pltpu.VMEM((N_FSDP * PADDED // 4, ROWS_DEV), BF16),
            pltpu.VMEM((ROWS_DEV, WIDTH), BF16),
            pltpu.VMEM((SLOTS * HEADS, WINDOW, WINDOW), BF16),
            pltpu.SemaphoreType.DMA((N_COPIES,)),
            pltpu.SemaphoreType.DMA((N_COPIES,)),
        ],
        compiler_params=pltpu.CompilerParams(
            collective_id=0, has_side_effects=True, vmem_limit_bytes=62 * MIB
        ),
        name="whole",
    )(shard, qkv, cot, live)


def body(query_key_value, cotangent, output_weight, layer_scale, tile_counts):
    device_id = lax.axis_index("dp") * N_FSDP + lax.axis_index("fsdp")
    own_tiles = tile_counts[device_id]
    live = (jnp.arange(8)[:, None] < own_tiles).astype(F32) * jnp.ones((1, 128), F32)
    scale = layer_scale.astype(F32)[None, :]
    scaled = (output_weight.astype(F32) * scale).astype(BF16)
    shard = jnp.pad(scaled.T, ((0, PADDED - SHARD), (0, 0)))

    grads, summed = whole(shard, query_key_value, cotangent, live)
    summed = summed[:SHARD].T.astype(F32)
    factor = 8.0 / math.sqrt(ROWS_DEV * N_FSDP * N_DP)
    grad_weight = factor * scale * summed
    grad_scale = factor * jnp.sum(output_weight.astype(F32) * summed, axis=0)
    return (grads, grad_weight, grad_scale)


def solution(mesh):
    in_specs = (P(("dp", "fsdp"), None), P(("dp", "fsdp"), None), P(None, "fsdp"), P("fsdp"), P())
    out_specs = (P(("dp", "fsdp"), None), P(None, "fsdp"), P("fsdp"))
    return jax.shard_map(body, mesh=mesh, in_specs=in_specs, out_specs=out_specs, check_vma=False)
```

```python
import functools
import math

import jax
import jax.numpy as jnp
from jax import lax
from jax.experimental import pallas as pl
from jax.experimental.pallas import tpu as pltpu
from jax.sharding import PartitionSpec as P

HEAD_DIM = 128
TILE = 257
SLOTS = 2
HEADS = 13
WIDTH = HEADS * HEAD_DIM
MODEL = 3200
SHARD = 100
PADDED = 112
N_FSDP = 32
N_DP = 8
ROWS_DEV = SLOTS * TILE
WINDOW = 258
STARTS = (0, 256)
COMMON = 640
PARITY = 512
PAIRS = (((0, 512), (512, 384)), ((896, 384), (1280, 384)))
SPLIT = 7
TOP = 64
BOTTOM = PADDED - TOP
PIECE = 16
MIB = 1024 * 1024
F32 = jnp.float32
BF16 = jnp.bfloat16
MESH = pl.DeviceIdType.MESH


def dot(a, b, dims):
    return lax.dot_general(a, b, (dims, ((), ())), preferred_element_type=F32)


def selection(tile, transposed):
    first = 128 * tile
    owner = first // PADDED
    base = owner * SHARD + jnp.minimum(first - owner * PADDED, SHARD - 1)
    source_tile = jnp.minimum(base // 128, MODEL // 128 - 2)
    shape = (128, 256) if transposed else (256, 128)
    line = (128, 1) if transposed else (1, 128)
    target = lax.broadcasted_iota(jnp.int32, line, 0 if transposed else 1) + first
    wanted = jnp.full(line, -1, jnp.int32)
    for step in range(3):
        index = owner + step
        inside = (target >= index * PADDED) & (target < index * PADDED + SHARD)
        place = target - index * (PADDED - SHARD) - source_tile * 128
        wanted = jnp.where(inside, place, wanted)
    source = lax.broadcasted_iota(jnp.int32, shape, 1 if transposed else 0)
    chosen = jnp.where(source == wanted, 1.0, 0.0)
    columns = pl.ds(pl.multiple_of(source_tile * 128, 128), 256)
    return chosen.astype(BF16), columns


def spread_cotangent(cot_ref, padded_ref):
    def one_tile(tile, carry):
        chooser, source = selection(tile, False)
        columns = pl.ds(pl.multiple_of(tile * 128, 128), 128)
        padded_ref[:, columns] = dot(cot_ref[:, source], chooser, ((1,), (0,))).astype(BF16)
        return carry

    lax.fori_loop(0, N_FSDP * PADDED // 128, one_tile, 0)


def with_ones(values):
    return jnp.concatenate([values, jnp.ones_like(values)], axis=1)


def store_window(ref, slot, columns, values, keep):
    start = STARTS[slot]
    if not keep:
        ref[start : start + WINDOW, columns] = values
    elif slot == 0:
        kept = ref[256:WINDOW, columns]
        row = lax.broadcasted_iota(jnp.int32, kept.shape, 0)
        ref[0:256, columns] = values[0:256]
        ref[256:WINDOW, columns] = jnp.where(row == 1, kept, values[256:WINDOW])
    else:
        kept = ref[256:272, columns]
        row = lax.broadcasted_iota(jnp.int32, kept.shape, 0)
        ref[256 : 256 + WINDOW, columns] = values
        ref[256:272, columns] = jnp.where(row == 0, kept, values[0:16])


def head_columns(third, head):
    return pl.ds(pl.multiple_of(third * WIDTH + head * HEAD_DIM, 128), HEAD_DIM)


def forward_heads(qkv_ref, live, attended_ref, probs_ref, first, last):
    factor = math.log2(math.e) / math.sqrt(HEAD_DIM)

    def one_head(head, carry):
        scores, powers, both = [], [], []
        for start in STARTS:
            rows = slice(start, start + WINDOW)
            queries = qkv_ref[rows, head_columns(0, head)]
            keys = qkv_ref[rows, head_columns(1, head)]
            scores.append(dot(queries, keys, ((1,), (1,))))
        for slot in range(SLOTS):
            out_of_tile = WINDOW - 1 if slot == 0 else 0
            column = lax.broadcasted_iota(jnp.int32, (1, WINDOW), 1)
            masked = jnp.where(column == out_of_tile, -1e30, scores[slot])
            top = jnp.max(masked, axis=1, keepdims=True)
            powers.append(jnp.exp2((masked - top) * factor))
        for slot, start in enumerate(STARTS):
            values = qkv_ref[start : start + WINDOW, head_columns(2, head)]
            both.append(dot(powers[slot].astype(BF16), with_ones(values), ((1,), (0,))))
        for slot in range(SLOTS):
            out_of_tile = WINDOW - 1 if slot == 0 else 0
            row = lax.broadcasted_iota(jnp.int32, (WINDOW, HEAD_DIM), 0)
            share = jnp.where(row == out_of_tile, 0.0, 1.0 / both[slot][:, HEAD_DIM:])
            for start in range(0, WINDOW, HEAD_DIM):
                size = min(HEAD_DIM, WINDOW - start)
                probs = powers[slot][:, start : start + size] * share[:, 0:size]
                probs_ref[slot * HEADS + head, :, start : start + size] = probs.astype(BF16)
            attended = jnp.where(live > slot, both[slot][:, :HEAD_DIM] * share, 0.0)
            store_window(
                attended_ref, slot, head_columns(0, head), attended.astype(BF16), slot == 1
            )
        return carry

    lax.fori_loop(first, last, one_head, 0)


def turn_cotangent(cot_ref, turned_ref):
    def one_tile(tile, carry):
        chooser, source = selection(tile, True)
        rows = pl.ds(pl.multiple_of(tile * 128, 128), 128)
        turned_ref[rows, :] = dot(chooser, cot_ref[:, source], ((1,), (1,))).astype(BF16)
        return carry

    lax.fori_loop(0, N_FSDP * PADDED // 128, one_tile, 0)


def weight_partials(turned_ref, attended_ref, partial_ref, lanes, first, last):
    height = N_FSDP * PADDED // 4

    def one_line(line, carry):
        rows = pl.ds(pl.multiple_of(line * height, height), height)
        for start in range(lanes.start, lanes.stop, 256):
            size = min(256, lanes.stop - start)
            columns = slice(start, start + size)
            sums = dot(turned_ref[rows, :], attended_ref[:, columns], ((1,), (0,)))
            partial_ref[line, :, :, :, columns] = sums.astype(BF16).reshape(4, 2, PADDED, size)
        return carry

    lax.fori_loop(first, last, one_line, 0)


def attended_grads(padded_ref, weight_ref, d_attended_ref, first, last):
    def one_block(columns, size):
        right = weight_ref[:, :, :, :, columns].reshape(N_FSDP * PADDED, size)
        d_attended_ref[:, columns] = dot(padded_ref[...], right, ((1,), (0,))).astype(BF16)

    def one_full(index, carry):
        one_block(pl.ds(pl.multiple_of(index * 256, 256), 256), 256)
        return carry

    lax.fori_loop(first, min(last, WIDTH // 256), one_full, 0)
    if last > WIDTH // 256 and WIDTH % 256:
        one_block(slice(WIDTH // 256 * 256, WIDTH), WIDTH % 256)


def backward_heads(qkv_ref, live, probs_ref, attended_ref, grad_ref, first, last):
    inverse = 1.0 / math.sqrt(HEAD_DIM)

    def one_head(head, carry):
        products, grads = [], []
        for start in STARTS:
            rows = slice(start, start + WINDOW)
            values = qkv_ref[rows, head_columns(2, head)]
            d_attended = grad_ref[rows, head_columns(0, head)]
            attended = attended_ref[rows, head_columns(0, head)]
            taken = -(d_attended.astype(F32) * attended.astype(F32))
            left = jnp.concatenate([d_attended, taken.astype(BF16)], axis=1)
            products.append(dot(left, with_ones(values), ((1,), (1,))))
        for slot, start in enumerate(STARTS):
            rows = slice(start, start + WINDOW)
            queries = qkv_ref[rows, head_columns(0, head)]
            keys = qkv_ref[rows, head_columns(1, head)]
            probs = probs_ref[slot * HEADS + head].astype(F32)
            d_scores = (probs * products[slot]).astype(BF16)
            grad_query = dot(d_scores, keys, ((1,), (0,))) * inverse
            grad_key = dot(d_scores, queries, ((0,), (0,))) * inverse
            grads.append(
                [jnp.where(live > slot, grad, 0.0).astype(BF16) for grad in (grad_query, grad_key)]
            )
        for slot in (1, 0):
            for third in (0, 1):
                store_window(grad_ref, slot, head_columns(third, head), grads[slot][third], True)
        return carry

    lax.fori_loop(first, last, one_head, 0)


class Copies:
    def __init__(self, send_sems, recv_sems):
        self.send_sems, self.recv_sems, self.count, self.made = send_sems, recv_sems, 0, []

    def start(self, source, target, device):
        copy = pltpu.make_async_remote_copy(
            src_ref=source,
            dst_ref=target,
            send_sem=self.send_sems.at[self.count],
            recv_sem=self.recv_sems.at[self.count],
            device_id=device,
            device_id_type=MESH,
        )
        copy.start()
        self.count += 1
        self.made.append(copy)
        return copy

    def finish(self):
        for copy in self.made:
            copy.wait_send()


class Place:
    def __init__(self):
        self.f = lax.axis_index("fsdp")
        self.z = lax.axis_index("dp")
        self.c = lax.rem(self.f, 2)
        chip = self.f // 2
        self.y = lax.rem(chip, 4)
        self.x = chip // 4

    def device(self, x, y, c):
        return (self.z, ((x * 4) + y) * 2 + c)

    def around(self, axis, steps):
        u = lax.rem((self.x if axis == 0 else self.y) + 4 + steps, 4)
        return u

    def neighbour(self, axis, steps):
        u = self.around(axis, steps)
        return self.device(u, self.y, self.c) if axis == 0 else self.device(self.x, u, self.c)

    def sibling(self):
        return self.device(self.x, self.y, 1 - self.c)

    def layer(self, steps):
        return lax.rem(self.z + steps, N_DP)

    def greet(self):
        barrier = pltpu.get_barrier_semaphore()
        others = [self.sibling()]
        for axis in (0, 1):
            for step in (1, -1):
                others.append(self.neighbour(axis, step))
        for step in range(1, N_DP):
            others.append((self.layer(step), self.f))
        for other in others:
            pl.semaphore_signal(barrier, inc=1, device_id=other, device_id_type=MESH)
        pl.semaphore_wait(barrier, len(others))


def pick(first, u, v):
    return (u, v) if first == 0 else (v, u)


class WeightGather:
    def __init__(self, place, copies, weight_ref):
        self.place, self.copies, self.weight = place, copies, weight_ref
        self.own = (place.x, place.y)
        self.last, self.shared, self.lifted = {}, [], {}
        parity = lax.rem(place.z, 2)
        self.table = (slice(0, COMMON), self.lanes_of(parity), self.lanes_of(1 - parity))

    def lanes_of(self, parity):
        return pl.ds(pl.multiple_of(COMMON + PARITY * parity, 128), PARITY)

    def block(self, half, x, y, rows=slice(0, PADDED)):
        return self.weight.at[x, y, self.place.c, rows, self.table[half]]

    def send(self, half, axis, step, x, y, rows=slice(0, PADDED)):
        ref = self.block(half, x, y, rows)
        return self.copies.start(ref, ref, self.place.neighbour(axis, step))

    def begin(self):
        self.first = {}
        self.second = {}
        for half in (0, 1):
            for step in (1, -1):
                self.first[half, step] = self.send(half, half, step, *self.own)
        for half in (0, 1):
            self.send_second(half, 0)

    def send_second(self, half, away):
        u, v = self.place.around(half, away), self.place.around(1 - half, 0)
        for step in (1, -1):
            self.second[half, away, step] = self.send(half, 1 - half, step, *pick(half, u, v))

    def middle(self):
        self.far = {}
        place = self.place
        for step in (1, -1):
            for half in (0, 1):
                self.first[half, step].wait_recv()
                u, v = place.around(half, -step), place.around(1 - half, 0)
                part = slice(0, TOP) if step == 1 else slice(TOP, PADDED)
                self.far[half, step] = self.send(half, half, step, *pick(half, u, v), part)
                self.send_second(half, -step)

    def farthest(self):
        for half in (0, 1):
            for step in (1, -1):
                self.far[half, step].wait_recv()
            self.send_second(half, 2)

    def spread(self, away):
        place = self.place
        for half in (0, 1):
            for step in (1, -1):
                self.second[half, away, step].wait_recv()
                u, v = place.around(half, away), place.around(1 - half, -step)
                part = slice(0, TOP) if step == 1 else slice(TOP, PADDED)
                self.last[half, away, step] = self.send(
                    half, 1 - half, step, *pick(half, u, v), part
                )

    def share(self, away):
        place = self.place
        for half in (1, 0):
            for step in (1, -1):
                self.last[half, away, step].wait_recv()
            u = place.around(half, away)
            if half == 1:
                self.lifted[away] = []
                for step, part in ((1, slice(0, 2)), (N_DP - 1, slice(2, 4))):
                    ref = self.weight.at[part, u, place.c, :, self.table[1]]
                    self.lifted[away].append(
                        self.copies.start(ref, ref, (place.layer(step), place.f))
                    )
            line = (u, slice(None)) if half == 0 else (slice(None), u)
            self.give(line, half)

    def give(self, line, half):
        ref = self.weight.at[*line, self.place.c, :, self.table[half]]
        self.shared.append(self.copies.start(ref, ref, self.place.sibling()))

    def cross(self, away):
        for copy in self.lifted[away]:
            copy.wait_recv()
        self.give((slice(None), self.place.around(1, away)), 2)

    def end(self):
        for copy in self.shared:
            copy.wait_recv()


class GradReduce:
    def __init__(
        self, place, copies, table, partial_ref, sums_ref, buffers, layers_ref, result_ref
    ):
        self.place, self.copies, self.table = place, copies, table
        self.whole = slice(table[0][0], table[1][0] + table[1][1])
        self.partial, self.sums, self.buffers = partial_ref, sums_ref, buffers
        self.layers, self.result = layers_ref, result_ref

    def line(self, half, away):
        u = self.place.around(half, away)
        return (u, slice(None)) if half == 0 else (slice(None), u)

    def lanes(self, half):
        return slice(self.table[half][0], self.table[half][0] + self.table[half][1])

    def begin(self):
        self.crossed = {}
        for away in (2, 1, -1, 0):
            for half in (0, 1):
                line, lanes = self.line(half, away), self.lanes(half)
                self.crossed[half, away] = self.copies.start(
                    self.partial.at[*line, 1 - self.place.c, :, lanes],
                    self.sums.at[*line, :, lanes],
                    self.place.sibling(),
                )

    def chunk(self, half, away, v):
        u = self.place.around(half, away)
        return pick(half, u, v)

    def add_own(self, half, away):
        self.crossed[half, away].wait_recv()
        lanes = self.lanes(half)

        def one(v, carry):
            x, y = self.chunk(half, away, v)
            self.sums[x, y, :, lanes] += self.partial[x, y, self.place.c, :, lanes]
            return carry

        lax.fori_loop(0, 4, one, 0)

    def group(self, half, away, first):
        u = self.place.around(half, away)
        part = slice(first, first + 2)
        return self.sums.at[*pick(half, u, part), :, self.lanes(half)]

    def sends_far(self):
        self.near, self.far = {}, {}
        place = self.place
        for half in (0, 1):
            self.add_own(half, 2)
            for step in (1, -1):
                self.far[half, step] = self.copies.start(
                    self.group(half, 2, 0 if step == 1 else 2),
                    self.buffers[half][0].at[0 if step == 1 else 1],
                    place.neighbour(half, step),
                )

    def sends_near(self):
        place = self.place
        for step in (1, -1):
            for half in (0, 1):
                self.add_own(half, step)
                other = 2 if step == 1 else 0
                self.near[half, step, 0] = self.copies.start(
                    self.group(half, step, other),
                    self.buffers[half][1].at[0 if step == 1 else 1, slice(other, other + 2)],
                    place.neighbour(half, step),
                )

    def own_line(self):
        for half in (0, 1):
            self.add_own(half, 0)

    def first_forward(self):
        place = self.place
        for step in (1, -1):
            for half in (0, 1):
                side, start = (0, 0) if step == 1 else (1, 2)
                self.far[half, step].wait_recv()
                lanes = self.lanes(half)
                arrived = self.buffers[half][0]

                def one(v, carry, half=half, side=side, start=start, lanes=lanes, arrived=arrived):
                    x, y = self.chunk(half, step, start + v)
                    self.sums[x, y, :, lanes] += arrived[side, v]
                    return carry

                lax.fori_loop(0, 2, one, 0)
                self.near[half, step, 1] = self.copies.start(
                    self.group(half, step, start),
                    self.buffers[half][1].at[side, slice(start, start + 2)],
                    place.neighbour(half, step),
                )

    def first_end(self):
        for half in (0, 1):
            for step in (1, -1):
                self.near[half, step, 0].wait_recv()
                self.near[half, step, 1].wait_recv()
            lanes = self.lanes(half)
            arrived = self.buffers[half][1]

            def one(v, carry, half=half, lanes=lanes, arrived=arrived):
                x, y = self.chunk(half, 0, v)
                total = self.sums[x, y, :, lanes].astype(F32)
                total += arrived[0, v].astype(F32) + arrived[1, v].astype(F32)
                self.sums[x, y, :, lanes] = total.astype(BF16)
                return carry

            lax.fori_loop(0, 4, one, 0)
            self.second_sends(half)

    def mine(self, half, away):
        place = self.place
        return pick(half, place.around(half, 0), place.around(1 - half, away))

    def second_sends(self, half):
        place, lanes = self.place, self.lanes(half)
        if half == 0:
            self.far2, self.near2 = {}, {}
        for step in (1, -1):
            side = 0 if step == 1 else 1
            rows = slice(0, TOP) if step == 1 else slice(TOP, PADDED)
            self.far2[half, step] = self.copies.start(
                self.sums.at[*self.mine(half, 2), rows, lanes],
                self.buffers[half][2].at[rows],
                place.neighbour(1 - half, step),
            )
        for step in (1, -1):
            side = 0 if step == 1 else 1
            rows = slice(TOP, PADDED) if step == 1 else slice(0, TOP)
            self.near2[half, step, 0] = self.copies.start(
                self.sums.at[*self.mine(half, step), rows, lanes],
                self.buffers[half][3].at[side, rows],
                place.neighbour(1 - half, step),
            )

    def second_forward(self):
        place = self.place
        for half in (0, 1):
            lanes = self.lanes(half)
            for step in (1, -1):
                side = 0 if step == 1 else 1
                rows = slice(0, TOP) if step == 1 else slice(TOP, PADDED)
                self.far2[half, step].wait_recv()
                x, y = self.mine(half, step)
                self.sums[x, y, rows, lanes] += self.buffers[half][2][rows]
                self.near2[half, step, 1] = self.copies.start(
                    self.sums.at[x, y, rows, lanes],
                    self.buffers[half][3].at[side, rows],
                    place.neighbour(1 - half, step),
                )

    def second_end(self):
        layers = self.layers
        layers[0, PADDED:128, :] = jnp.zeros((128 - PADDED, layers.shape[2]), BF16)
        for half in (0, 1):
            lanes = self.lanes(half)
            for step in (1, -1):
                self.near2[half, step, 0].wait_recv()
                self.near2[half, step, 1].wait_recv()
            x, y = self.mine(half, 0)
            arrived = self.buffers[half][3]
            total = self.sums[x, y, :, lanes].astype(F32)
            total += arrived[0].astype(F32) + arrived[1].astype(F32)
            local = slice(lanes.start - self.whole.start, lanes.stop - self.whole.start)
            layers[0, 0:PADDED, local] = total.astype(BF16)

    def piece(self, z):
        return pl.ds(pl.multiple_of(z * PIECE, PIECE), PIECE)

    def layer_sends(self):
        place = self.place
        self.up = [
            self.copies.start(
                self.layers.at[0, self.piece(place.layer(step))],
                self.layers.at[1, slice(step * PIECE, step * PIECE + PIECE)],
                (place.layer(step), place.f),
            )
            for step in range(1, N_DP)
        ]

    def layer_sums(self):
        place = self.place
        own = self.piece(place.z)
        total = self.layers[0, own, :].astype(F32)
        for step in range(1, N_DP):
            self.up[step - 1].wait_recv()
            total += self.layers[1, step * PIECE : step * PIECE + PIECE, :].astype(F32)
        self.result[own, self.whole] = total.astype(BF16)
        self.down = [
            self.copies.start(
                self.result.at[own, self.whole],
                self.result.at[own, self.whole],
                (place.layer(step), place.f),
            )
            for step in range(1, N_DP)
        ]

    def end(self):
        for copy in self.down:
            copy.wait_recv()


N_COPIES = 48 + 12 + 2 * (8 + 12 + 12 + 14)


def whole_kernel(counts_ref, matrix_ref, gain_ref, qkv_ref, cot_ref, *refs):
    grad_ref, grad_weight_ref, grad_scale_ref = refs[:3]
    weight_ref, partial_ref, sums_ref, result_ref, padded_ref, turned_ref = refs[3:9]
    attended_ref, probs_ref, send_sems, recv_sems, load_sem = refs[9:14]
    buffers = refs[14:]
    held_ref = grad_ref
    load = pltpu.make_async_copy(cot_ref, grad_ref.at[:, 0:MODEL], load_sem)
    load.start()
    place = Place()
    copies = Copies(send_sems, recv_sems)
    gain = gain_ref[:, 0:1]
    shard = (matrix_ref[...].astype(F32) * gain).astype(BF16)
    weight_ref[place.x, place.y, place.c, 0:SHARD] = shard
    weight_ref[place.x, place.y, place.c, SHARD:PADDED] = jnp.zeros(
        (PADDED - SHARD, WIDTH), BF16
    )
    place.greet()
    live = jnp.full((1, HEAD_DIM), counts_ref[place.z * N_FSDP + place.f], jnp.int32)
    gather = WeightGather(place, copies, weight_ref)
    early, late = [
        GradReduce(
            place, copies, PAIRS[i], partial_ref, sums_ref,
            (buffers[9 * i : 9 * i + 4], buffers[9 * i + 4 : 9 * i + 8]), buffers[9 * i + 8],
            result_ref,
        )
        for i in (0, 1)
    ]

    def forward(first, last):
        forward_heads(qkv_ref, live, attended_ref, probs_ref, first, last)

    def backward(first, last):
        backward_heads(qkv_ref, live, probs_ref, attended_ref, grad_ref, first, last)

    def d_attended(first, last):
        attended_grads(padded_ref, weight_ref, grad_ref, first, last)

    def partials(lanes, first, last):
        weight_partials(turned_ref, attended_ref, partial_ref, lanes, first, last)

    gather.begin()
    forward(0, 3)
    gather.middle()
    forward(3, SPLIT)
    gather.farthest()
    load.wait()
    turn_cotangent(held_ref, turned_ref)
    gather.spread(0)
    partials(early.whole, 0, 2)
    gather.spread(-1)
    gather.spread(1)
    partials(early.whole, 2, 4)
    early.begin()
    gather.share(0)
    gather.spread(2)
    forward(SPLIT, 10)
    gather.share(-1)
    gather.share(1)
    early.sends_far()
    forward(10, HEADS)
    early.sends_near()
    gather.share(2)
    partials(late.whole, 0, 2)
    early.own_line()
    early.first_forward()
    gather.cross(0)
    gather.cross(-1)
    partials(late.whole, 2, 4)
    late.begin()
    gather.cross(1)
    spread_cotangent(held_ref, padded_ref)
    late.sends_far()
    early.first_end()
    gather.cross(2)
    late.sends_near()
    late.own_line()
    gather.end()
    d_attended(0, 2)
    late.first_forward()
    early.second_forward()
    d_attended(2, 4)
    early.second_end()
    early.layer_sends()
    late.first_end()
    d_attended(4, 7)
    late.second_forward()
    backward(0, 3)
    early.layer_sums()
    late.second_end()
    late.layer_sends()
    backward(3, 9)
    late.layer_sums()
    backward(9, HEADS)
    early.end()
    late.end()
    summed = result_ref[0:SHARD, :].astype(F32)
    factor = 8.0 / math.sqrt(ROWS_DEV * N_FSDP * N_DP)
    grad_weight_ref[...] = factor * gain * summed
    total = factor * jnp.sum(matrix_ref[...].astype(F32) * summed, axis=1, keepdims=True)
    grad_scale_ref[...] = jnp.broadcast_to(total, (SHARD, 128))
    copies.finish()


def exchange_buffers():
    shapes = []
    for table in PAIRS:
        for _, size in table:
            shapes += [
                pltpu.VMEM((2, 2, PADDED, size), BF16),
                pltpu.VMEM((2, 4, PADDED, size), BF16),
                pltpu.VMEM((PADDED, size), BF16),
                pltpu.VMEM((2, PADDED, size), BF16),
            ]
        shapes.append(pltpu.VMEM((2, 128, table[0][1] + table[1][1]), BF16))
    return shapes


VMEM = pl.BlockSpec(memory_space=pltpu.VMEM)


def whole(counts, matrix, gain, qkv, cot):
    return pl.pallas_call(
        whole_kernel,
        out_shape=(
            jax.ShapeDtypeStruct((ROWS_DEV, 2 * WIDTH), BF16),
            jax.ShapeDtypeStruct((SHARD, WIDTH), F32),
            jax.ShapeDtypeStruct((SHARD, 128), F32),
        ),
        in_specs=[pl.BlockSpec(memory_space=pltpu.SMEM)] + [VMEM] * 3 + [pl.BlockSpec(memory_space=pl.ANY)],
        out_specs=[VMEM] * 3,
        scratch_shapes=[
            pltpu.VMEM((4, 4, 2, PADDED, WIDTH), BF16),
            pltpu.VMEM((4, 4, 2, PADDED, WIDTH), BF16),
            pltpu.VMEM((4, 4, PADDED, WIDTH), BF16),
            pltpu.VMEM((128, WIDTH), BF16),
            pltpu.VMEM((ROWS_DEV, N_FSDP * PADDED), BF16),
            pltpu.VMEM((N_FSDP * PADDED, ROWS_DEV), BF16),
            pltpu.VMEM((ROWS_DEV, WIDTH), BF16),
            pltpu.VMEM((SLOTS * HEADS, WINDOW, WINDOW), BF16),
            pltpu.SemaphoreType.DMA((N_COPIES,)),
            pltpu.SemaphoreType.DMA((N_COPIES,)),
            pltpu.SemaphoreType.DMA,
        ]
        + exchange_buffers(),
        compiler_params=pltpu.CompilerParams(
            collective_id=0, has_side_effects=True, vmem_limit_bytes=62 * MIB
        ),
        name="whole",
    )(counts, matrix, gain, qkv, cot)


def body(query_key_value, cotangent, output_weight, layer_scale, tile_counts):
    gain = jnp.broadcast_to(layer_scale.astype(F32)[:, None], (SHARD, 128))
    grads, grad_weight, grad_scale = whole(
        tile_counts, output_weight.T, gain, query_key_value, cotangent
    )
    return (grads, grad_weight.T, grad_scale[:, 0])


def solution(mesh):
    in_specs = (P(("dp", "fsdp"), None), P(("dp", "fsdp"), None), P(None, "fsdp"), P("fsdp"), P())
    out_specs = (P(("dp", "fsdp"), None), P(None, "fsdp"), P("fsdp"))
    return jax.shard_map(body, mesh=mesh, in_specs=in_specs, out_specs=out_specs, check_vma=False)
```

```python
import functools
import math

import jax
import jax.numpy as jnp
from jax import lax
from jax.experimental import pallas as pl
from jax.experimental.pallas import tpu as pltpu
from jax.sharding import PartitionSpec as P

HEAD_DIM = 128
TILE = 257
SLOTS = 2
HEADS = 13
WIDTH = HEADS * HEAD_DIM
MODEL = 3200
SHARD = 100
PADDED = 112
N_FSDP = 32
N_DP = 8
ROWS_DEV = SLOTS * TILE
WINDOW = 258
STARTS = (0, 256)
FIRST = 640
SECOND = 768
PARITY = 256
PAIRS = (((0, 512), (512, 384)), ((896, 384), (1280, 384)))
SPLIT = 7
TOP = 64
BOTTOM = PADDED - TOP
PIECE = 16
MIB = 1024 * 1024
F32 = jnp.float32
BF16 = jnp.bfloat16
MESH = pl.DeviceIdType.MESH


def dot(a, b, dims):
    return lax.dot_general(a, b, (dims, ((), ())), preferred_element_type=F32)


def selection(tile, transposed):
    first = 128 * tile
    owner = first // PADDED
    base = owner * SHARD + jnp.minimum(first - owner * PADDED, SHARD - 1)
    source_tile = jnp.minimum(base // 128, MODEL // 128 - 2)
    shape = (128, 256) if transposed else (256, 128)
    line = (128, 1) if transposed else (1, 128)
    target = lax.broadcasted_iota(jnp.int32, line, 0 if transposed else 1) + first
    wanted = jnp.full(line, -1, jnp.int32)
    for step in range(3):
        index = owner + step
        inside = (target >= index * PADDED) & (target < index * PADDED + SHARD)
        place = target - index * (PADDED - SHARD) - source_tile * 128
        wanted = jnp.where(inside, place, wanted)
    source = lax.broadcasted_iota(jnp.int32, shape, 1 if transposed else 0)
    chosen = jnp.where(source == wanted, 1.0, 0.0)
    columns = pl.ds(pl.multiple_of(source_tile * 128, 128), 256)
    return chosen.astype(BF16), columns


def spread_cotangent(cot_ref, padded_ref):
    def one_tile(tile, carry):
        chooser, source = selection(tile, False)
        columns = pl.ds(pl.multiple_of(tile * 128, 128), 128)
        padded_ref[:, columns] = dot(cot_ref[:, source], chooser, ((1,), (0,))).astype(BF16)
        return carry

    lax.fori_loop(0, N_FSDP * PADDED // 128, one_tile, 0)


def with_ones(values):
    return jnp.concatenate([values, jnp.ones_like(values)], axis=1)


def store_window(ref, slot, columns, values, keep):
    start = STARTS[slot]
    if not keep:
        ref[start : start + WINDOW, columns] = values
    elif slot == 0:
        kept = ref[256:WINDOW, columns]
        row = lax.broadcasted_iota(jnp.int32, kept.shape, 0)
        ref[0:256, columns] = values[0:256]
        ref[256:WINDOW, columns] = jnp.where(row == 1, kept, values[256:WINDOW])
    else:
        kept = ref[256:272, columns]
        row = lax.broadcasted_iota(jnp.int32, kept.shape, 0)
        ref[256 : 256 + WINDOW, columns] = values
        ref[256:272, columns] = jnp.where(row == 0, kept, values[0:16])


def head_columns(third, head):
    return pl.ds(pl.multiple_of(third * WIDTH + head * HEAD_DIM, 128), HEAD_DIM)


def forward_heads(qkv_ref, live, attended_ref, probs_ref, first, last):
    factor = math.log2(math.e) / math.sqrt(HEAD_DIM)

    def one_head(head, carry):
        scores, powers, both = [], [], []
        for start in STARTS:
            rows = slice(start, start + WINDOW)
            queries = qkv_ref[rows, head_columns(0, head)]
            keys = qkv_ref[rows, head_columns(1, head)]
            scores.append(dot(queries, keys, ((1,), (1,))))
        for slot in range(SLOTS):
            out_of_tile = WINDOW - 1 if slot == 0 else 0
            column = lax.broadcasted_iota(jnp.int32, (1, WINDOW), 1)
            masked = jnp.where(column == out_of_tile, -1e30, scores[slot])
            top = jnp.max(masked, axis=1, keepdims=True)
            powers.append(jnp.exp2((masked - top) * factor))
        for slot, start in enumerate(STARTS):
            values = qkv_ref[start : start + WINDOW, head_columns(2, head)]
            both.append(dot(powers[slot].astype(BF16), with_ones(values), ((1,), (0,))))
        for slot in range(SLOTS):
            out_of_tile = WINDOW - 1 if slot == 0 else 0
            row = lax.broadcasted_iota(jnp.int32, (WINDOW, HEAD_DIM), 0)
            share = jnp.where(row == out_of_tile, 0.0, 1.0 / both[slot][:, HEAD_DIM:])
            for start in range(0, WINDOW, HEAD_DIM):
                size = min(HEAD_DIM, WINDOW - start)
                probs = powers[slot][:, start : start + size] * share[:, 0:size]
                probs_ref[slot * HEADS + head, :, start : start + size] = probs.astype(BF16)
            attended = jnp.where(live > slot, both[slot][:, :HEAD_DIM] * share, 0.0)
            store_window(
                attended_ref, slot, head_columns(0, head), attended.astype(BF16), slot == 1
            )
        return carry

    lax.fori_loop(first, last, one_head, 0)


def turn_cotangent(cot_ref, turned_ref):
    def one_tile(tile, carry):
        chooser, source = selection(tile, True)
        rows = pl.ds(pl.multiple_of(tile * 128, 128), 128)
        turned_ref[rows, :] = dot(chooser, cot_ref[:, source], ((1,), (1,))).astype(BF16)
        return carry

    lax.fori_loop(0, N_FSDP * PADDED // 128, one_tile, 0)


def weight_partials(turned_ref, attended_ref, partial_ref, lanes, first, last):
    height = N_FSDP * PADDED // 4

    def one_line(line, carry):
        rows = pl.ds(pl.multiple_of(line * height, height), height)
        for start in range(lanes.start, lanes.stop, 256):
            size = min(256, lanes.stop - start)
            columns = slice(start, start + size)
            sums = dot(turned_ref[rows, :], attended_ref[:, columns], ((1,), (0,)))
            partial_ref[line, :, :, :, columns] = sums.astype(BF16).reshape(4, 2, PADDED, size)
        return carry

    lax.fori_loop(first, last, one_line, 0)


def attended_grads(padded_ref, weight_ref, d_attended_ref, first, last):
    def one_block(columns, size):
        right = weight_ref[:, :, :, :, columns].reshape(N_FSDP * PADDED, size)
        d_attended_ref[:, columns] = dot(padded_ref[...], right, ((1,), (0,))).astype(BF16)

    def one_full(index, carry):
        one_block(pl.ds(pl.multiple_of(index * 256, 256), 256), 256)
        return carry

    lax.fori_loop(first, min(last, WIDTH // 256), one_full, 0)
    if last > WIDTH // 256 and WIDTH % 256:
        one_block(slice(WIDTH // 256 * 256, WIDTH), WIDTH % 256)


def backward_heads(qkv_ref, live, probs_ref, attended_ref, grad_ref, first, last):
    inverse = 1.0 / math.sqrt(HEAD_DIM)

    def one_head(head, carry):
        products, grads = [], []
        for start in STARTS:
            rows = slice(start, start + WINDOW)
            values = qkv_ref[rows, head_columns(2, head)]
            d_attended = grad_ref[rows, head_columns(0, head)]
            attended = attended_ref[rows, head_columns(0, head)]
            taken = -(d_attended.astype(F32) * attended.astype(F32))
            left = jnp.concatenate([d_attended, taken.astype(BF16)], axis=1)
            products.append(dot(left, with_ones(values), ((1,), (1,))))
        for slot, start in enumerate(STARTS):
            rows = slice(start, start + WINDOW)
            queries = qkv_ref[rows, head_columns(0, head)]
            keys = qkv_ref[rows, head_columns(1, head)]
            probs = probs_ref[slot * HEADS + head].astype(F32)
            d_scores = (probs * products[slot]).astype(BF16)
            grad_query = dot(d_scores, keys, ((1,), (0,))) * inverse
            grad_key = dot(d_scores, queries, ((0,), (0,))) * inverse
            grads.append(
                [jnp.where(live > slot, grad, 0.0).astype(BF16) for grad in (grad_query, grad_key)]
            )
        for slot in (1, 0):
            for third in (0, 1):
                store_window(grad_ref, slot, head_columns(third, head), grads[slot][third], True)
        return carry

    lax.fori_loop(first, last, one_head, 0)


class Copies:
    def __init__(self, send_sems, recv_sems):
        self.send_sems, self.recv_sems, self.count, self.made = send_sems, recv_sems, 0, []

    def start(self, source, target, device):
        copy = pltpu.make_async_remote_copy(
            src_ref=source,
            dst_ref=target,
            send_sem=self.send_sems.at[self.count],
            recv_sem=self.recv_sems.at[self.count],
            device_id=device,
            device_id_type=MESH,
        )
        copy.start()
        self.count += 1
        self.made.append(copy)
        return copy

    def finish(self):
        for copy in self.made:
            copy.wait_send()


class Place:
    def __init__(self):
        self.f = lax.axis_index("fsdp")
        self.z = lax.axis_index("dp")
        self.c = lax.rem(self.f, 2)
        chip = self.f // 2
        self.y = lax.rem(chip, 4)
        self.x = chip // 4

    def device(self, x, y, c):
        return (self.z, ((x * 4) + y) * 2 + c)

    def around(self, axis, steps):
        u = lax.rem((self.x if axis == 0 else self.y) + 4 + steps, 4)
        return u

    def neighbour(self, axis, steps):
        u = self.around(axis, steps)
        return self.device(u, self.y, self.c) if axis == 0 else self.device(self.x, u, self.c)

    def sibling(self):
        return self.device(self.x, self.y, 1 - self.c)

    def layer(self, steps):
        return lax.rem(self.z + steps, N_DP)

    def greet(self):
        barrier = pltpu.get_barrier_semaphore()
        others = [self.sibling()]
        for axis in (0, 1):
            for step in (1, -1):
                others.append(self.neighbour(axis, step))
        for step in range(1, N_DP):
            others.append((self.layer(step), self.f))
        for other in others:
            pl.semaphore_signal(barrier, inc=1, device_id=other, device_id_type=MESH)
        pl.semaphore_wait(barrier, len(others))


def pick(first, u, v):
    return (u, v) if first == 0 else (v, u)


class WeightGather:
    def __init__(self, place, copies, weight_ref):
        self.place, self.copies, self.weight = place, copies, weight_ref
        self.own = (place.x, place.y)
        self.last, self.shared, self.lifted = {}, [], {}
        parity = lax.rem(place.z, 2)
        self.table = (
            slice(WIDTH - FIRST, WIDTH),
            self.lanes_of(PARITY * parity, SECOND),
            self.lanes_of(SECOND * parity, PARITY),
            self.lanes_of(SECOND * (1 - parity), PARITY),
        )

    def lanes_of(self, start, size):
        return pl.ds(pl.multiple_of(start, 128), size)

    def block(self, half, x, y, rows=slice(0, PADDED)):
        return self.weight.at[x, y, self.place.c, rows, self.table[half]]

    def send(self, half, axis, step, x, y, rows=slice(0, PADDED)):
        ref = self.block(half, x, y, rows)
        return self.copies.start(ref, ref, self.place.neighbour(axis, step))

    def begin(self):
        self.first = {}
        self.second = {}
        for half in (0, 1):
            for step in (1, -1):
                self.first[half, step] = self.send(half, half, step, *self.own)
        for half in (0, 1):
            self.send_second(half, 0)

    def send_second(self, half, away):
        u, v = self.place.around(half, away), self.place.around(1 - half, 0)
        for step in (1, -1):
            self.second[half, away, step] = self.send(half, 1 - half, step, *pick(half, u, v))

    def middle(self):
        self.far = {}
        place = self.place
        for step in (1, -1):
            for half in (0, 1):
                self.first[half, step].wait_recv()
                u, v = place.around(half, -step), place.around(1 - half, 0)
                part = slice(0, TOP) if step == 1 else slice(TOP, PADDED)
                self.far[half, step] = self.send(half, half, step, *pick(half, u, v), part)
                self.send_second(half, -step)

    def farthest(self):
        for half in (0, 1):
            for step in (1, -1):
                self.far[half, step].wait_recv()
            self.send_second(half, 2)

    def spread(self, away):
        place = self.place
        for half in (0, 1):
            for step in (1, -1):
                self.second[half, away, step].wait_recv()
                u, v = place.around(half, away), place.around(1 - half, -step)
                part = slice(0, TOP) if step == 1 else slice(TOP, PADDED)
                self.last[half, away, step] = self.send(
                    half, 1 - half, step, *pick(half, u, v), part
                )

    def share(self, away):
        place = self.place
        for half in (1, 0):
            for step in (1, -1):
                self.last[half, away, step].wait_recv()
            u = place.around(half, away)
            if half == 1:
                self.lifted[away] = []
                for step, part in ((1, slice(0, 2)), (N_DP - 1, slice(2, 4))):
                    ref = self.weight.at[part, u, place.c, :, self.table[2]]
                    self.lifted[away].append(
                        self.copies.start(ref, ref, (place.layer(step), place.f))
                    )
            line = (u, slice(None)) if half == 0 else (slice(None), u)
            self.give(line, half)

    def give(self, line, half):
        ref = self.weight.at[*line, self.place.c, :, self.table[half]]
        self.shared.append(self.copies.start(ref, ref, self.place.sibling()))

    def cross(self, away):
        for copy in self.lifted[away]:
            copy.wait_recv()
        self.give((slice(None), self.place.around(1, away)), 3)

    def end(self):
        for copy in self.shared:
            copy.wait_recv()


class GradReduce:
    def __init__(
        self, place, copies, table, partial_ref, sums_ref, buffers, layers_ref, result_ref
    ):
        self.place, self.copies, self.table = place, copies, table
        self.whole = slice(table[0][0], table[1][0] + table[1][1])
        self.partial, self.sums, self.buffers = partial_ref, sums_ref, buffers
        self.layers, self.result = layers_ref, result_ref

    def line(self, half, away):
        u = self.place.around(half, away)
        return (u, slice(None)) if half == 0 else (slice(None), u)

    def lanes(self, half):
        return slice(self.table[half][0], self.table[half][0] + self.table[half][1])

    def begin(self):
        self.crossed = {}
        for away in (2, 1, -1, 0):
            for half in (0, 1):
                line, lanes = self.line(half, away), self.lanes(half)
                self.crossed[half, away] = self.copies.start(
                    self.partial.at[*line, 1 - self.place.c, :, lanes],
                    self.sums.at[*line, :, lanes],
                    self.place.sibling(),
                )

    def chunk(self, half, away, v):
        u = self.place.around(half, away)
        return pick(half, u, v)

    def add_own(self, half, away):
        self.crossed[half, away].wait_recv()
        lanes = self.lanes(half)

        def one(v, carry):
            x, y = self.chunk(half, away, v)
            self.sums[x, y, :, lanes] += self.partial[x, y, self.place.c, :, lanes]
            return carry

        lax.fori_loop(0, 4, one, 0)

    def group(self, half, away, first):
        u = self.place.around(half, away)
        part = slice(first, first + 2)
        return self.sums.at[*pick(half, u, part), :, self.lanes(half)]

    def sends_far(self):
        self.near, self.far = {}, {}
        place = self.place
        for half in (0, 1):
            self.add_own(half, 2)
            for step in (1, -1):
                self.far[half, step] = self.copies.start(
                    self.group(half, 2, 0 if step == 1 else 2),
                    self.buffers[half][0].at[0 if step == 1 else 1],
                    place.neighbour(half, step),
                )

    def sends_near(self):
        place = self.place
        for step in (1, -1):
            for half in (0, 1):
                self.add_own(half, step)
                other = 2 if step == 1 else 0
                self.near[half, step, 0] = self.copies.start(
                    self.group(half, step, other),
                    self.buffers[half][1].at[0 if step == 1 else 1, slice(other, other + 2)],
                    place.neighbour(half, step),
                )

    def own_line(self):
        for half in (0, 1):
            self.add_own(half, 0)

    def first_forward(self):
        place = self.place
        for step in (1, -1):
            for half in (0, 1):
                side, start = (0, 0) if step == 1 else (1, 2)
                self.far[half, step].wait_recv()
                lanes = self.lanes(half)
                arrived = self.buffers[half][0]

                def one(v, carry, half=half, side=side, start=start, lanes=lanes, arrived=arrived):
                    x, y = self.chunk(half, step, start + v)
                    self.sums[x, y, :, lanes] += arrived[side, v]
                    return carry

                lax.fori_loop(0, 2, one, 0)
                self.near[half, step, 1] = self.copies.start(
                    self.group(half, step, start),
                    self.buffers[half][1].at[side, slice(start, start + 2)],
                    place.neighbour(half, step),
                )

    def first_end(self):
        for half in (0, 1):
            for step in (1, -1):
                self.near[half, step, 0].wait_recv()
                self.near[half, step, 1].wait_recv()
            lanes = self.lanes(half)
            arrived = self.buffers[half][1]

            def one(v, carry, half=half, lanes=lanes, arrived=arrived):
                x, y = self.chunk(half, 0, v)
                total = self.sums[x, y, :, lanes].astype(F32)
                total += arrived[0, v].astype(F32) + arrived[1, v].astype(F32)
                self.sums[x, y, :, lanes] = total.astype(BF16)
                return carry

            lax.fori_loop(0, 4, one, 0)
            self.second_sends(half)

    def mine(self, half, away):
        place = self.place
        return pick(half, place.around(half, 0), place.around(1 - half, away))

    def second_sends(self, half):
        place, lanes = self.place, self.lanes(half)
        if half == 0:
            self.far2, self.near2 = {}, {}
        for step in (1, -1):
            side = 0 if step == 1 else 1
            rows = slice(0, TOP) if step == 1 else slice(TOP, PADDED)
            self.far2[half, step] = self.copies.start(
                self.sums.at[*self.mine(half, 2), rows, lanes],
                self.buffers[half][2].at[rows],
                place.neighbour(1 - half, step),
            )
        for step in (1, -1):
            side = 0 if step == 1 else 1
            rows = slice(TOP, PADDED) if step == 1 else slice(0, TOP)
            self.near2[half, step, 0] = self.copies.start(
                self.sums.at[*self.mine(half, step), rows, lanes],
                self.buffers[half][3].at[side, rows],
                place.neighbour(1 - half, step),
            )

    def second_forward(self):
        place = self.place
        for half in (0, 1):
            lanes = self.lanes(half)
            for step in (1, -1):
                side = 0 if step == 1 else 1
                rows = slice(0, TOP) if step == 1 else slice(TOP, PADDED)
                self.far2[half, step].wait_recv()
                x, y = self.mine(half, step)
                self.sums[x, y, rows, lanes] += self.buffers[half][2][rows]
                self.near2[half, step, 1] = self.copies.start(
                    self.sums.at[x, y, rows, lanes],
                    self.buffers[half][3].at[side, rows],
                    place.neighbour(1 - half, step),
                )

    def second_end(self):
        layers = self.layers
        layers[0, PADDED:128, :] = jnp.zeros((128 - PADDED, layers.shape[2]), BF16)
        for half in (0, 1):
            lanes = self.lanes(half)
            for step in (1, -1):
                self.near2[half, step, 0].wait_recv()
                self.near2[half, step, 1].wait_recv()
            x, y = self.mine(half, 0)
            arrived = self.buffers[half][3]
            total = self.sums[x, y, :, lanes].astype(F32)
            total += arrived[0].astype(F32) + arrived[1].astype(F32)
            local = slice(lanes.start - self.whole.start, lanes.stop - self.whole.start)
            layers[0, 0:PADDED, local] = total.astype(BF16)

    def piece(self, z):
        return pl.ds(pl.multiple_of(z * PIECE, PIECE), PIECE)

    def layer_sends(self):
        place = self.place
        self.up = [
            self.copies.start(
                self.layers.at[0, self.piece(place.layer(step))],
                self.layers.at[1, slice(step * PIECE, step * PIECE + PIECE)],
                (place.layer(step), place.f),
            )
            for step in range(1, N_DP)
        ]

    def layer_sums(self):
        place = self.place
        own = self.piece(place.z)
        total = self.layers[0, own, :].astype(F32)
        for step in range(1, N_DP):
            self.up[step - 1].wait_recv()
            total += self.layers[1, step * PIECE : step * PIECE + PIECE, :].astype(F32)
        self.result[own, self.whole] = total.astype(BF16)
        self.down = [
            self.copies.start(
                self.result.at[own, self.whole],
                self.result.at[own, self.whole],
                (place.layer(step), place.f),
            )
            for step in range(1, N_DP)
        ]

    def end(self):
        for copy in self.down:
            copy.wait_recv()


N_COPIES = 48 + 12 + 2 * (8 + 12 + 12 + 14)


def whole_kernel(counts_ref, matrix_ref, gain_ref, qkv_ref, cot_ref, *refs):
    grad_ref, grad_weight_ref, grad_scale_ref = refs[:3]
    weight_ref, partial_ref, sums_ref, result_ref, padded_ref, turned_ref = refs[3:9]
    attended_ref, probs_ref, send_sems, recv_sems, load_sem = refs[9:14]
    buffers = refs[14:]
    held_ref = grad_ref
    load = pltpu.make_async_copy(cot_ref, grad_ref.at[:, 0:MODEL], load_sem)
    load.start()
    place = Place()
    copies = Copies(send_sems, recv_sems)
    gain = gain_ref[:, 0:1]
    shard = (matrix_ref[...].astype(F32) * gain).astype(BF16)
    weight_ref[place.x, place.y, place.c, 0:SHARD] = shard
    weight_ref[place.x, place.y, place.c, SHARD:PADDED] = jnp.zeros(
        (PADDED - SHARD, WIDTH), BF16
    )
    place.greet()
    live = jnp.full((1, HEAD_DIM), counts_ref[place.z * N_FSDP + place.f], jnp.int32)
    gather = WeightGather(place, copies, weight_ref)
    early, late = [
        GradReduce(
            place, copies, PAIRS[i], partial_ref, sums_ref,
            (buffers[9 * i : 9 * i + 4], buffers[9 * i + 4 : 9 * i + 8]), buffers[9 * i + 8],
            result_ref,
        )
        for i in (0, 1)
    ]

    def forward(first, last):
        forward_heads(qkv_ref, live, attended_ref, probs_ref, first, last)

    def backward(first, last):
        backward_heads(qkv_ref, live, probs_ref, attended_ref, grad_ref, first, last)

    def d_attended(first, last):
        attended_grads(padded_ref, weight_ref, grad_ref, first, last)

    def partials(lanes, first, last):
        weight_partials(turned_ref, attended_ref, partial_ref, lanes, first, last)

    gather.begin()
    forward(0, 3)
    gather.middle()
    forward(3, SPLIT)
    gather.farthest()
    load.wait()
    turn_cotangent(held_ref, turned_ref)
    gather.spread(0)
    partials(early.whole, 0, 2)
    gather.spread(-1)
    gather.spread(1)
    partials(early.whole, 2, 4)
    early.begin()
    gather.share(0)
    gather.spread(2)
    forward(SPLIT, 10)
    gather.share(-1)
    gather.share(1)
    early.sends_far()
    forward(10, HEADS)
    early.sends_near()
    gather.share(2)
    partials(late.whole, 0, 2)
    early.own_line()
    early.first_forward()
    gather.cross(0)
    partials(late.whole, 2, 4)
    late.begin()
    gather.cross(-1)
    spread_cotangent(held_ref, padded_ref)
    late.sends_far()
    gather.cross(1)
    late.sends_near()
    early.first_end()
    gather.cross(2)
    late.own_line()
    early.second_forward()
    late.first_forward()
    gather.end()
    d_attended(0, 2)
    early.second_end()
    early.layer_sends()
    d_attended(2, 4)
    late.first_end()
    early.layer_sums()
    d_attended(4, 7)
    late.second_forward()
    backward(0, 3)
    late.second_end()
    late.layer_sends()
    backward(3, 8)
    late.layer_sums()
    backward(8, HEADS)
    early.end()
    late.end()
    summed = result_ref[0:SHARD, :].astype(F32)
    factor = 8.0 / math.sqrt(ROWS_DEV * N_FSDP * N_DP)
    grad_weight_ref[...] = factor * gain * summed
    total = factor * jnp.sum(matrix_ref[...].astype(F32) * summed, axis=1, keepdims=True)
    grad_scale_ref[...] = jnp.broadcast_to(total, (SHARD, 128))
    copies.finish()


def exchange_buffers():
    shapes = []
    for table in PAIRS:
        for _, size in table:
            shapes += [
                pltpu.VMEM((2, 2, PADDED, size), BF16),
                pltpu.VMEM((2, 4, PADDED, size), BF16),
                pltpu.VMEM((PADDED, size), BF16),
                pltpu.VMEM((2, PADDED, size), BF16),
            ]
        shapes.append(pltpu.VMEM((2, 128, table[0][1] + table[1][1]), BF16))
    return shapes


VMEM = pl.BlockSpec(memory_space=pltpu.VMEM)


def whole(counts, matrix, gain, qkv, cot):
    return pl.pallas_call(
        whole_kernel,
        out_shape=(
            jax.ShapeDtypeStruct((ROWS_DEV, 2 * WIDTH), BF16),
            jax.ShapeDtypeStruct((SHARD, WIDTH), F32),
            jax.ShapeDtypeStruct((SHARD, 128), F32),
        ),
        in_specs=[pl.BlockSpec(memory_space=pltpu.SMEM)] + [VMEM] * 3 + [pl.BlockSpec(memory_space=pl.ANY)],
        out_specs=[VMEM] * 3,
        scratch_shapes=[
            pltpu.VMEM((4, 4, 2, PADDED, WIDTH), BF16),
            pltpu.VMEM((4, 4, 2, PADDED, WIDTH), BF16),
            pltpu.VMEM((4, 4, PADDED, WIDTH), BF16),
            pltpu.VMEM((128, WIDTH), BF16),
            pltpu.VMEM((ROWS_DEV, N_FSDP * PADDED), BF16),
            pltpu.VMEM((N_FSDP * PADDED, ROWS_DEV), BF16),
            pltpu.VMEM((ROWS_DEV, WIDTH), BF16),
            pltpu.VMEM((SLOTS * HEADS, WINDOW, WINDOW), BF16),
            pltpu.SemaphoreType.DMA((N_COPIES,)),
            pltpu.SemaphoreType.DMA((N_COPIES,)),
            pltpu.SemaphoreType.DMA,
        ]
        + exchange_buffers(),
        compiler_params=pltpu.CompilerParams(
            collective_id=0, has_side_effects=True, vmem_limit_bytes=62 * MIB
        ),
        name="whole",
    )(counts, matrix, gain, qkv, cot)


def body(query_key_value, cotangent, output_weight, layer_scale, tile_counts):
    gain = jnp.broadcast_to(layer_scale.astype(F32)[:, None], (SHARD, 128))
    grads, grad_weight, grad_scale = whole(
        tile_counts, output_weight.T, gain, query_key_value, cotangent
    )
    return (grads, grad_weight.T, grad_scale[:, 0])


def solution(mesh):
    in_specs = (P(("dp", "fsdp"), None), P(("dp", "fsdp"), None), P(None, "fsdp"), P("fsdp"), P())
    out_specs = (P(("dp", "fsdp"), None), P(None, "fsdp"), P("fsdp"))
    return jax.shard_map(body, mesh=mesh, in_specs=in_specs, out_specs=out_specs, check_vma=False)
```

```python
import functools
import math

import jax
import jax.numpy as jnp
from jax import lax
from jax.experimental import pallas as pl
from jax.experimental.pallas import tpu as pltpu
from jax.sharding import PartitionSpec as P

HEAD_DIM = 128
TILE = 257
SLOTS = 2
HEADS = 13
WIDTH = HEADS * HEAD_DIM
MODEL = 3200
SHARD = 100
PADDED = 112
N_FSDP = 32
N_DP = 8
ROWS_DEV = SLOTS * TILE
WINDOW = 258
STARTS = (0, 256)
FIRST = 640
SECOND = 768
PARITY = 256
PAIRS = (((0, 512), (512, 384)), ((896, 384), (1280, 384)))
SPLIT = 7
TOP = 64
BOTTOM = PADDED - TOP
PIECE = 16
MIB = 1024 * 1024
F32 = jnp.float32
BF16 = jnp.bfloat16
MESH = pl.DeviceIdType.MESH


def dot(a, b, dims):
    return lax.dot_general(a, b, (dims, ((), ())), preferred_element_type=F32)


def selection(tile, transposed):
    first = 128 * tile
    owner = first // PADDED
    base = owner * SHARD + jnp.minimum(first - owner * PADDED, SHARD - 1)
    source_tile = jnp.minimum(base // 128, MODEL // 128 - 2)
    shape = (128, 256) if transposed else (256, 128)
    line = (128, 1) if transposed else (1, 128)
    target = lax.broadcasted_iota(jnp.int32, line, 0 if transposed else 1) + first
    wanted = jnp.full(line, -1, jnp.int32)
    for step in range(3):
        index = owner + step
        inside = (target >= index * PADDED) & (target < index * PADDED + SHARD)
        place = target - index * (PADDED - SHARD) - source_tile * 128
        wanted = jnp.where(inside, place, wanted)
    source = lax.broadcasted_iota(jnp.int32, shape, 1 if transposed else 0)
    chosen = jnp.where(source == wanted, 1.0, 0.0)
    columns = pl.ds(pl.multiple_of(source_tile * 128, 128), 256)
    return chosen.astype(BF16), columns


def spread_cotangent(cot_ref, padded_ref):
    def one_tile(tile, carry):
        chooser, source = selection(tile, False)
        columns = pl.ds(pl.multiple_of(tile * 128, 128), 128)
        padded_ref[:, columns] = dot(cot_ref[:, source], chooser, ((1,), (0,))).astype(BF16)
        return carry

    lax.fori_loop(0, N_FSDP * PADDED // 128, one_tile, 0)


def with_ones(values):
    return jnp.concatenate([values, jnp.ones_like(values)], axis=1)


def store_window(ref, slot, columns, values, keep):
    start = STARTS[slot]
    if not keep:
        ref[start : start + WINDOW, columns] = values
    elif slot == 0:
        kept = ref[256:WINDOW, columns]
        row = lax.broadcasted_iota(jnp.int32, kept.shape, 0)
        ref[0:256, columns] = values[0:256]
        ref[256:WINDOW, columns] = jnp.where(row == 1, kept, values[256:WINDOW])
    else:
        kept = ref[256:272, columns]
        row = lax.broadcasted_iota(jnp.int32, kept.shape, 0)
        ref[256 : 256 + WINDOW, columns] = values
        ref[256:272, columns] = jnp.where(row == 0, kept, values[0:16])


def head_columns(third, head):
    return pl.ds(pl.multiple_of(third * WIDTH + head * HEAD_DIM, 128), HEAD_DIM)


def forward_heads(qkv_ref, live, attended_ref, probs_ref, first, last):
    factor = math.log2(math.e) / math.sqrt(HEAD_DIM)

    def one_head(head, carry):
        scores, powers, both = [], [], []
        for start in STARTS:
            rows = slice(start, start + WINDOW)
            queries = qkv_ref[rows, head_columns(0, head)]
            keys = qkv_ref[rows, head_columns(1, head)]
            scores.append(dot(queries, keys, ((1,), (1,))))
        for slot in range(SLOTS):
            out_of_tile = WINDOW - 1 if slot == 0 else 0
            column = lax.broadcasted_iota(jnp.int32, (1, WINDOW), 1)
            masked = jnp.where(column == out_of_tile, -1e30, scores[slot])
            top = jnp.max(masked, axis=1, keepdims=True)
            powers.append(jnp.exp2((masked - top) * factor))
        for slot, start in enumerate(STARTS):
            values = qkv_ref[start : start + WINDOW, head_columns(2, head)]
            both.append(dot(powers[slot].astype(BF16), with_ones(values), ((1,), (0,))))
        for slot in range(SLOTS):
            out_of_tile = WINDOW - 1 if slot == 0 else 0
            row = lax.broadcasted_iota(jnp.int32, (WINDOW, HEAD_DIM), 0)
            share = jnp.where(row == out_of_tile, 0.0, 1.0 / both[slot][:, HEAD_DIM:])
            for start in range(0, WINDOW, HEAD_DIM):
                size = min(HEAD_DIM, WINDOW - start)
                probs = powers[slot][:, start : start + size] * share[:, 0:size]
                probs_ref[slot * HEADS + head, :, start : start + size] = probs.astype(BF16)
            attended = jnp.where(live > slot, both[slot][:, :HEAD_DIM] * share, 0.0)
            store_window(
                attended_ref, slot, head_columns(0, head), attended.astype(BF16), slot == 1
            )
        return carry

    lax.fori_loop(first, last, one_head, 0)


def turn_cotangent(cot_ref, turned_ref):
    def one_tile(tile, carry):
        chooser, source = selection(tile, True)
        rows = pl.ds(pl.multiple_of(tile * 128, 128), 128)
        turned_ref[rows, :] = dot(chooser, cot_ref[:, source], ((1,), (1,))).astype(BF16)
        return carry

    lax.fori_loop(0, N_FSDP * PADDED // 128, one_tile, 0)


def weight_partials(turned_ref, attended_ref, partial_ref, lanes, first, last):
    height = N_FSDP * PADDED // 4

    def one_line(line, carry):
        rows = pl.ds(pl.multiple_of(line * height, height), height)
        for start in range(lanes.start, lanes.stop, 256):
            size = min(256, lanes.stop - start)
            columns = slice(start, start + size)
            sums = dot(turned_ref[rows, :], attended_ref[:, columns], ((1,), (0,)))
            partial_ref[line, :, :, :, columns] = sums.astype(BF16).reshape(4, 2, PADDED, size)
        return carry

    lax.fori_loop(first, last, one_line, 0)


def attended_grads(padded_ref, weight_ref, d_attended_ref, first, last):
    def one_block(columns, size):
        right = weight_ref[:, :, :, :, columns].reshape(N_FSDP * PADDED, size)
        d_attended_ref[:, columns] = dot(padded_ref[...], right, ((1,), (0,))).astype(BF16)

    def one_full(index, carry):
        one_block(pl.ds(pl.multiple_of(index * 256, 256), 256), 256)
        return carry

    lax.fori_loop(first, min(last, WIDTH // 256), one_full, 0)
    if last > WIDTH // 256 and WIDTH % 256:
        one_block(slice(WIDTH // 256 * 256, WIDTH), WIDTH % 256)


def backward_heads(qkv_ref, live, probs_ref, attended_ref, grad_ref, first, last):
    inverse = 1.0 / math.sqrt(HEAD_DIM)

    def one_head(head, carry):
        products, grads = [], []
        for start in STARTS:
            rows = slice(start, start + WINDOW)
            values = qkv_ref[rows, head_columns(2, head)]
            d_attended = grad_ref[rows, head_columns(0, head)]
            attended = attended_ref[rows, head_columns(0, head)]
            taken = -(d_attended.astype(F32) * attended.astype(F32))
            left = jnp.concatenate([d_attended, taken.astype(BF16)], axis=1)
            products.append(dot(left, with_ones(values), ((1,), (1,))))
        for slot, start in enumerate(STARTS):
            rows = slice(start, start + WINDOW)
            queries = qkv_ref[rows, head_columns(0, head)]
            keys = qkv_ref[rows, head_columns(1, head)]
            probs = probs_ref[slot * HEADS + head].astype(F32)
            d_scores = (probs * products[slot]).astype(BF16)
            grad_query = dot(d_scores, keys, ((1,), (0,))) * inverse
            grad_key = dot(d_scores, queries, ((0,), (0,))) * inverse
            grads.append(
                [jnp.where(live > slot, grad, 0.0).astype(BF16) for grad in (grad_query, grad_key)]
            )
        for slot in (1, 0):
            for third in (0, 1):
                store_window(grad_ref, slot, head_columns(third, head), grads[slot][third], True)
        return carry

    lax.fori_loop(first, last, one_head, 0)


class Copies:
    def __init__(self, send_sems, recv_sems):
        self.send_sems, self.recv_sems, self.count, self.made = send_sems, recv_sems, 0, []

    def start(self, source, target, device):
        copy = pltpu.make_async_remote_copy(
            src_ref=source,
            dst_ref=target,
            send_sem=self.send_sems.at[self.count],
            recv_sem=self.recv_sems.at[self.count],
            device_id=device,
            device_id_type=MESH,
        )
        copy.start()
        self.count += 1
        self.made.append(copy)
        return copy

    def finish(self):
        for copy in self.made:
            copy.wait_send()


class Place:
    def __init__(self):
        self.f = lax.axis_index("fsdp")
        self.z = lax.axis_index("dp")
        self.c = lax.rem(self.f, 2)
        chip = self.f // 2
        self.y = lax.rem(chip, 4)
        self.x = chip // 4

    def device(self, x, y, c):
        return (self.z, ((x * 4) + y) * 2 + c)

    def around(self, axis, steps):
        u = lax.rem((self.x if axis == 0 else self.y) + 4 + steps, 4)
        return u

    def neighbour(self, axis, steps):
        u = self.around(axis, steps)
        return self.device(u, self.y, self.c) if axis == 0 else self.device(self.x, u, self.c)

    def sibling(self):
        return self.device(self.x, self.y, 1 - self.c)

    def layer(self, steps):
        return lax.rem(self.z + steps, N_DP)

    def greet(self):
        barrier = pltpu.get_barrier_semaphore()
        others = [self.sibling()]
        for axis in (0, 1):
            for step in (1, -1):
                others.append(self.neighbour(axis, step))
        for step in range(1, N_DP):
            others.append((self.layer(step), self.f))
        for other in others:
            pl.semaphore_signal(barrier, inc=1, device_id=other, device_id_type=MESH)
        pl.semaphore_wait(barrier, len(others))


def pick(first, u, v):
    return (u, v) if first == 0 else (v, u)


class WeightGather:
    def __init__(self, place, copies, weight_ref):
        self.place, self.copies, self.weight = place, copies, weight_ref
        self.own = (place.x, place.y)
        self.last, self.shared, self.lifted = {}, [], {}
        parity = lax.rem(place.z, 2)
        self.table = (
            slice(WIDTH - FIRST, WIDTH),
            self.lanes_of(PARITY * parity, SECOND),
            self.lanes_of(SECOND * parity, PARITY),
            self.lanes_of(SECOND * (1 - parity), PARITY),
        )

    def lanes_of(self, start, size):
        return pl.ds(pl.multiple_of(start, 128), size)

    def block(self, half, x, y, rows=slice(0, PADDED)):
        return self.weight.at[x, y, self.place.c, rows, self.table[half]]

    def send(self, half, axis, step, x, y, rows=slice(0, PADDED)):
        ref = self.block(half, x, y, rows)
        return self.copies.start(ref, ref, self.place.neighbour(axis, step))

    def begin(self):
        self.first = {}
        self.second = {}
        for half in (0, 1):
            for step in (1, -1):
                self.first[half, step] = self.send(half, half, step, *self.own)
        for half in (0, 1):
            self.send_second(half, 0)

    def send_second(self, half, away):
        u, v = self.place.around(half, away), self.place.around(1 - half, 0)
        for step in (1, -1):
            self.second[half, away, step] = self.send(half, 1 - half, step, *pick(half, u, v))

    def middle(self):
        self.far = {}
        place = self.place
        for step in (1, -1):
            for half in (0, 1):
                self.first[half, step].wait_recv()
                u, v = place.around(half, -step), place.around(1 - half, 0)
                part = slice(0, TOP) if step == 1 else slice(TOP, PADDED)
                self.far[half, step] = self.send(half, half, step, *pick(half, u, v), part)
                self.send_second(half, -step)

    def farthest(self):
        for half in (0, 1):
            for step in (1, -1):
                self.far[half, step].wait_recv()
            self.send_second(half, 2)

    def spread(self, away):
        place = self.place
        for half in (0, 1):
            for step in (1, -1):
                self.second[half, away, step].wait_recv()
                u, v = place.around(half, away), place.around(1 - half, -step)
                part = slice(0, TOP) if step == 1 else slice(TOP, PADDED)
                self.last[half, away, step] = self.send(
                    half, 1 - half, step, *pick(half, u, v), part
                )

    def share(self, away):
        place = self.place
        for half in (1, 0):
            for step in (1, -1):
                self.last[half, away, step].wait_recv()
            u = place.around(half, away)
            if half == 1:
                self.lifted[away] = []
                for step, part in ((1, slice(0, 2)), (N_DP - 1, slice(2, 4))):
                    ref = self.weight.at[part, u, place.c, :, self.table[2]]
                    self.lifted[away].append(
                        self.copies.start(ref, ref, (place.layer(step), place.f))
                    )
            line = (u, slice(None)) if half == 0 else (slice(None), u)
            self.give(line, half)

    def give(self, line, half):
        ref = self.weight.at[*line, self.place.c, :, self.table[half]]
        self.shared.append(self.copies.start(ref, ref, self.place.sibling()))

    def cross(self, away):
        for copy in self.lifted[away]:
            copy.wait_recv()
        self.give((slice(None), self.place.around(1, away)), 3)

    def end(self):
        for copy in self.shared:
            copy.wait_recv()


class GradReduce:
    def __init__(
        self, place, copies, table, partial_ref, sums_ref, buffers, layers_ref, result_ref
    ):
        self.place, self.copies, self.table = place, copies, table
        self.whole = slice(table[0][0], table[1][0] + table[1][1])
        self.partial, self.sums, self.buffers = partial_ref, sums_ref, buffers
        self.layers, self.result = layers_ref, result_ref

    def line(self, half, away):
        u = self.place.around(half, away)
        return (u, slice(None)) if half == 0 else (slice(None), u)

    def lanes(self, half):
        return slice(self.table[half][0], self.table[half][0] + self.table[half][1])

    def begin(self):
        self.crossed = {}
        for away in (2, 1, -1, 0):
            for half in (0, 1):
                line, lanes = self.line(half, away), self.lanes(half)
                self.crossed[half, away] = self.copies.start(
                    self.partial.at[*line, 1 - self.place.c, :, lanes],
                    self.sums.at[*line, :, lanes],
                    self.place.sibling(),
                )

    def chunk(self, half, away, v):
        u = self.place.around(half, away)
        return pick(half, u, v)

    def add_own(self, half, away):
        self.crossed[half, away].wait_recv()
        lanes = self.lanes(half)

        def one(v, carry):
            x, y = self.chunk(half, away, v)
            self.sums[x, y, :, lanes] += self.partial[x, y, self.place.c, :, lanes]
            return carry

        lax.fori_loop(0, 4, one, 0)

    def group(self, half, away, first):
        u = self.place.around(half, away)
        part = slice(first, first + 2)
        return self.sums.at[*pick(half, u, part), :, self.lanes(half)]

    def sends_far(self):
        self.near, self.far = {}, {}
        place = self.place
        for half in (0, 1):
            self.add_own(half, 2)
            for step in (1, -1):
                self.far[half, step] = self.copies.start(
                    self.group(half, 2, 0 if step == 1 else 2),
                    self.buffers[half][0].at[0 if step == 1 else 1],
                    place.neighbour(half, step),
                )

    def sends_near(self):
        place = self.place
        for step in (1, -1):
            for half in (0, 1):
                self.add_own(half, step)
                other = 2 if step == 1 else 0
                self.near[half, step, 0] = self.copies.start(
                    self.group(half, step, other),
                    self.buffers[half][1].at[0 if step == 1 else 1, slice(other, other + 2)],
                    place.neighbour(half, step),
                )

    def own_line(self):
        for half in (0, 1):
            self.add_own(half, 0)

    def first_forward(self):
        place = self.place
        for step in (1, -1):
            for half in (0, 1):
                side, start = (0, 0) if step == 1 else (1, 2)
                self.far[half, step].wait_recv()
                lanes = self.lanes(half)
                arrived = self.buffers[half][0]

                def one(v, carry, half=half, side=side, start=start, lanes=lanes, arrived=arrived):
                    x, y = self.chunk(half, step, start + v)
                    self.sums[x, y, :, lanes] += arrived[side, v]
                    return carry

                lax.fori_loop(0, 2, one, 0)
                self.near[half, step, 1] = self.copies.start(
                    self.group(half, step, start),
                    self.buffers[half][1].at[side, slice(start, start + 2)],
                    place.neighbour(half, step),
                )

    def first_end(self):
        for half in (0, 1):
            for step in (1, -1):
                self.near[half, step, 0].wait_recv()
                self.near[half, step, 1].wait_recv()
            lanes = self.lanes(half)
            arrived = self.buffers[half][1]

            def one(v, carry, half=half, lanes=lanes, arrived=arrived):
                x, y = self.chunk(half, 0, v)
                total = self.sums[x, y, :, lanes].astype(F32)
                total += arrived[0, v].astype(F32) + arrived[1, v].astype(F32)
                self.sums[x, y, :, lanes] = total.astype(BF16)
                return carry

            lax.fori_loop(0, 4, one, 0)
            self.second_sends(half)

    def mine(self, half, away):
        place = self.place
        return pick(half, place.around(half, 0), place.around(1 - half, away))

    def second_sends(self, half):
        place, lanes = self.place, self.lanes(half)
        if half == 0:
            self.far2, self.near2 = {}, {}
        for step in (1, -1):
            side = 0 if step == 1 else 1
            rows = slice(0, TOP) if step == 1 else slice(TOP, PADDED)
            self.far2[half, step] = self.copies.start(
                self.sums.at[*self.mine(half, 2), rows, lanes],
                self.buffers[half][2].at[rows],
                place.neighbour(1 - half, step),
            )
        for step in (1, -1):
            side = 0 if step == 1 else 1
            rows = slice(TOP, PADDED) if step == 1 else slice(0, TOP)
            self.near2[half, step, 0] = self.copies.start(
                self.sums.at[*self.mine(half, step), rows, lanes],
                self.buffers[half][3].at[side, rows],
                place.neighbour(1 - half, step),
            )

    def second_forward(self):
        place = self.place
        for half in (0, 1):
            lanes = self.lanes(half)
            for step in (1, -1):
                side = 0 if step == 1 else 1
                rows = slice(0, TOP) if step == 1 else slice(TOP, PADDED)
                self.far2[half, step].wait_recv()
                x, y = self.mine(half, step)
                self.sums[x, y, rows, lanes] += self.buffers[half][2][rows]
                self.near2[half, step, 1] = self.copies.start(
                    self.sums.at[x, y, rows, lanes],
                    self.buffers[half][3].at[side, rows],
                    place.neighbour(1 - half, step),
                )

    def second_end(self):
        layers = self.layers
        layers[0, PADDED:128, :] = jnp.zeros((128 - PADDED, layers.shape[2]), BF16)
        for half in (0, 1):
            lanes = self.lanes(half)
            for step in (1, -1):
                self.near2[half, step, 0].wait_recv()
                self.near2[half, step, 1].wait_recv()
            x, y = self.mine(half, 0)
            arrived = self.buffers[half][3]
            total = self.sums[x, y, :, lanes].astype(F32)
            total += arrived[0].astype(F32) + arrived[1].astype(F32)
            local = slice(lanes.start - self.whole.start, lanes.stop - self.whole.start)
            layers[0, 0:PADDED, local] = total.astype(BF16)

    def piece(self, z):
        return pl.ds(pl.multiple_of(z * PIECE, PIECE), PIECE)

    def layer_sends(self):
        place = self.place
        self.up = [
            self.copies.start(
                self.layers.at[0, self.piece(place.layer(step))],
                self.layers.at[1, slice(step * PIECE, step * PIECE + PIECE)],
                (place.layer(step), place.f),
            )
            for step in range(1, N_DP)
        ]

    def layer_sums(self):
        place = self.place
        own = self.piece(place.z)
        total = self.layers[0, own, :].astype(F32)
        for step in range(1, N_DP):
            self.up[step - 1].wait_recv()
            total += self.layers[1, step * PIECE : step * PIECE + PIECE, :].astype(F32)
        self.result[own, self.whole] = total.astype(BF16)
        self.down = [
            self.copies.start(
                self.result.at[own, self.whole],
                self.result.at[own, self.whole],
                (place.layer(step), place.f),
            )
            for step in range(1, N_DP)
        ]

    def end(self):
        for copy in self.down:
            copy.wait_recv()


N_COPIES = 48 + 12 + 2 * (8 + 12 + 12 + 14)


def whole_kernel(counts_ref, matrix_ref, gain_ref, qkv_ref, cot_ref, *refs):
    grad_ref, grad_weight_ref, grad_scale_ref = refs[:3]
    weight_ref, partial_ref, sums_ref, result_ref, padded_ref, turned_ref = refs[3:9]
    attended_ref, probs_ref, send_sems, recv_sems, load_sem = refs[9:14]
    buffers = refs[14:]
    held_ref = grad_ref
    load = pltpu.make_async_copy(cot_ref, grad_ref.at[:, 0:MODEL], load_sem)
    load.start()
    place = Place()
    copies = Copies(send_sems, recv_sems)
    gain = gain_ref[:, 0:1]
    shard = (matrix_ref[...].astype(F32) * gain).astype(BF16)
    weight_ref[place.x, place.y, place.c, 0:SHARD] = shard
    weight_ref[place.x, place.y, place.c, SHARD:PADDED] = jnp.zeros(
        (PADDED - SHARD, WIDTH), BF16
    )
    place.greet()
    live = jnp.full((1, HEAD_DIM), counts_ref[place.z * N_FSDP + place.f], jnp.int32)
    gather = WeightGather(place, copies, weight_ref)
    early, late = [
        GradReduce(
            place, copies, PAIRS[i], partial_ref, sums_ref,
            (buffers[9 * i : 9 * i + 4], buffers[9 * i + 4 : 9 * i + 8]), buffers[9 * i + 8],
            result_ref,
        )
        for i in (0, 1)
    ]

    def forward(first, last):
        forward_heads(qkv_ref, live, attended_ref, probs_ref, first, last)

    def backward(first, last):
        backward_heads(qkv_ref, live, probs_ref, attended_ref, grad_ref, first, last)

    def d_attended(first, last):
        attended_grads(padded_ref, weight_ref, grad_ref, first, last)

    def partials(lanes, first, last):
        weight_partials(turned_ref, attended_ref, partial_ref, lanes, first, last)

    gather.begin()
    forward(0, 3)
    gather.middle()
    forward(3, SPLIT)
    gather.farthest()
    load.wait()
    turn_cotangent(held_ref, turned_ref)
    gather.spread(0)
    partials(early.whole, 0, 2)
    gather.spread(-1)
    gather.spread(1)
    partials(early.whole, 2, 4)
    early.begin()
    gather.share(0)
    gather.spread(2)
    forward(SPLIT, 10)
    gather.share(-1)
    gather.share(1)
    early.sends_far()
    forward(10, HEADS)
    early.sends_near()
    gather.share(2)
    partials(late.whole, 0, 2)
    early.own_line()
    early.first_forward()
    gather.cross(0)
    gather.cross(-1)
    partials(late.whole, 2, 4)
    late.begin()
    gather.cross(1)
    spread_cotangent(held_ref, padded_ref)
    late.sends_far()
    early.first_end()
    gather.cross(2)
    late.sends_near()
    late.own_line()
    gather.end()
    d_attended(0, 2)
    late.first_forward()
    early.second_forward()
    d_attended(2, 4)
    early.second_end()
    early.layer_sends()
    late.first_end()
    d_attended(4, 7)
    late.second_forward()
    backward(0, 3)
    early.layer_sums()
    late.second_end()
    late.layer_sends()
    backward(3, 9)
    late.layer_sums()
    backward(9, HEADS)
    early.end()
    late.end()
    summed = result_ref[0:SHARD, :].astype(F32)
    factor = 8.0 / math.sqrt(ROWS_DEV * N_FSDP * N_DP)
    grad_weight_ref[...] = factor * gain * summed
    total = factor * jnp.sum(matrix_ref[...].astype(F32) * summed, axis=1, keepdims=True)
    grad_scale_ref[...] = jnp.broadcast_to(total, (SHARD, 128))
    copies.finish()


def exchange_buffers():
    shapes = []
    for table in PAIRS:
        for _, size in table:
            shapes += [
                pltpu.VMEM((2, 2, PADDED, size), BF16),
                pltpu.VMEM((2, 4, PADDED, size), BF16),
                pltpu.VMEM((PADDED, size), BF16),
                pltpu.VMEM((2, PADDED, size), BF16),
            ]
        shapes.append(pltpu.VMEM((2, 128, table[0][1] + table[1][1]), BF16))
    return shapes


VMEM = pl.BlockSpec(memory_space=pltpu.VMEM)


def whole(counts, matrix, gain, qkv, cot):
    return pl.pallas_call(
        whole_kernel,
        out_shape=(
            jax.ShapeDtypeStruct((ROWS_DEV, 2 * WIDTH), BF16),
            jax.ShapeDtypeStruct((SHARD, WIDTH), F32),
            jax.ShapeDtypeStruct((SHARD, 128), F32),
        ),
        in_specs=[pl.BlockSpec(memory_space=pltpu.SMEM)] + [VMEM] * 3 + [pl.BlockSpec(memory_space=pl.ANY)],
        out_specs=[VMEM] * 3,
        scratch_shapes=[
            pltpu.VMEM((4, 4, 2, PADDED, WIDTH), BF16),
            pltpu.VMEM((4, 4, 2, PADDED, WIDTH), BF16),
            pltpu.VMEM((4, 4, PADDED, WIDTH), BF16),
            pltpu.VMEM((128, WIDTH), BF16),
            pltpu.VMEM((ROWS_DEV, N_FSDP * PADDED), BF16),
            pltpu.VMEM((N_FSDP * PADDED, ROWS_DEV), BF16),
            pltpu.VMEM((ROWS_DEV, WIDTH), BF16),
            pltpu.VMEM((SLOTS * HEADS, WINDOW, WINDOW), BF16),
            pltpu.SemaphoreType.DMA((N_COPIES,)),
            pltpu.SemaphoreType.DMA((N_COPIES,)),
            pltpu.SemaphoreType.DMA,
        ]
        + exchange_buffers(),
        compiler_params=pltpu.CompilerParams(
            collective_id=0, has_side_effects=True, vmem_limit_bytes=62 * MIB
        ),
        name="whole",
    )(counts, matrix, gain, qkv, cot)


def body(query_key_value, cotangent, output_weight, layer_scale, tile_counts):
    gain = jnp.broadcast_to(layer_scale.astype(F32)[:, None], (SHARD, 128))
    grads, grad_weight, grad_scale = whole(
        tile_counts, output_weight.T, gain, query_key_value, cotangent
    )
    return (grads, grad_weight.T, grad_scale[:, 0])


def solution(mesh):
    in_specs = (P(("dp", "fsdp"), None), P(("dp", "fsdp"), None), P(None, "fsdp"), P("fsdp"), P())
    out_specs = (P(("dp", "fsdp"), None), P(None, "fsdp"), P("fsdp"))
    return jax.shard_map(body, mesh=mesh, in_specs=in_specs, out_specs=out_specs, check_vma=False)
```
